32 devices in a mesh: groups: 2 (over x), ept: 8 (over z, y), exp: 2 (over core).
Axes of the slice: x: 2, y: 2, z: 4, core: 2. Of those that a mesh axis runs over, the one named last changes fastest.
Arguments:
- tokens: bfloat16 [4096, 6144], P(('groups', 'ept', 'exp')), parts along dimension 0, may hold values from -6 to 6
- expert_ids: int32 [4096, 2], P(('groups', 'ept', 'exp')), parts along dimension 0, may hold values from 0 to 7, as said below
- route_weights: float32 [4096, 2], P(('groups', 'ept', 'exp')), parts along dimension 0, may hold values from 0.1 to 1
- w_gate: bfloat16 [2, 6144, 8192], P('exp', None, 'ept'), may hold values from -0.078125 to 0.078125
- w_up: bfloat16 [2, 6144, 8192], P('exp', None, 'ept'), may hold values from -0.078125 to 0.078125
- w_down: bfloat16 [2, 8192, 6144], P('exp', 'ept'), may hold values from -0.0625 to 0.0625
Outputs:
- mixed_out: bfloat16 [4096, 6144], P(('groups', 'ept', 'exp')), parts along dimension 0
The draws below stay inside these ranges and needn't reach their ends.
There are 2 independent parts, one for each index of `groups`. The reference program is written for one: setup_inputs(seed, part) draws one part's arguments, and reference() takes and returns one part's arrays. A program takes and returns all parts, laid end to end along the dimension named above; an argument that names none is the same for every part. Nothing has to cross between parts.
Inputs may be any that keep to these rules, and one draw needn't show every extreme that they name: `expert_ids`: the 2 experts named in one row differ.
All inputs are finite; a program needn't handle non-finite values.
Results may differ from the reference program's by a relative error of at most 0.013.
Values may be sent and summed in bfloat16 or wider, within the bound.
No kernel may reach another device: no remote copies, remote signals or barrier semaphores. Data moves between devices by JAX's collectives and lax.ppermute only.
A program may use at most 128 MiB of HBM per device.

```python
import math
import jax
import jax.numpy as jnp
from jax import lax

D = 6144
FF = 8192
ROUTED = 8
TOP = 2
TOK_DEV = 128
EXPERTS = 2
CAP = 16
TOKENS = 2048
N_EPT = 8


def draw_expert_ids(key, part):
    key = jax.random.fold_in(key, 17)
    block_count = TOKENS // TOK_DEV
    subkeys = jax.random.split(key, 7)
    favored = jax.random.randint(subkeys[0], (), 0, EXPERTS)
    partner = (favored + jax.random.randint(subkeys[1], (), 1, EXPERTS)) % EXPERTS
    ranking = jax.vmap(lambda subkey: jax.random.permutation(subkey, TOK_DEV))(jax.random.split(subkeys[2], block_count))
    partner_rows = jax.random.randint(subkeys[3], (block_count, 1), CAP // 4, CAP + 1)
    hot_rows = CAP + CAP // 2
    spare_count = ROUTED - EXPERTS
    first_pick = jax.random.randint(subkeys[4], (block_count, TOK_DEV), 0, spare_count)
    second_pick = (first_pick + jax.random.randint(subkeys[5], (block_count, TOK_DEV), 1, spare_count)) % spare_count + EXPERTS
    first_pick = first_pick + EXPERTS
    in_favored = ranking < hot_rows
    in_partner = (ranking >= hot_rows) & (ranking < hot_rows + partner_rows)
    window_pick = jnp.where(in_favored, favored, partner)
    leading = jnp.where(in_favored | in_partner, window_pick, first_pick)
    flipped = jax.random.randint(subkeys[6], (block_count, TOK_DEV), 0, 2) == 1
    column_a = jnp.where(flipped, second_pick, leading)
    column_b = jnp.where(flipped, leading, second_pick)
    return jnp.stack([column_a, column_b], axis=-1).reshape(TOKENS, 2).astype(jnp.int32)


def steps_of(own_key, dims, cuts, smallest, top_value):
    def one(position, parts):
        steps = jax.random.uniform(jax.random.fold_in(jax.random.fold_in(own_key, 6), position), (parts,), jnp.float32, smallest / len(cuts), top_value / len(cuts))
        return jnp.repeat(jnp.exp(steps), dims[position] // parts).reshape((-1,) + (1,) * (len(dims) - position - 1))

    factor_of = one(*cuts[0])
    for cut in cuts[1:]:
        factor_of = factor_of * one(*cut)
    return factor_of


def scatter_about(key, shape, deviation, most, shards=(), kind=jnp.bfloat16):
    level = steps_of(key, shape, shards, -0.22, 0.18) if shards else 1.0
    result = jax.random.normal(key, shape, jnp.float32) * deviation * level
    return jnp.minimum(jnp.maximum(result, -most), most).astype(kind)


def setup_inputs(seed: int = 0, part: int = 0) -> dict:
    splits = jax.random.split(jax.random.key(seed), 7)
    own_keys = jax.random.split(jax.random.fold_in(splits[6], part), 7)
    return {
        "tokens": scatter_about(own_keys[0], (TOKENS, D), 1.0, 6.0, ((0, 16),)),
        "expert_ids": draw_expert_ids(jax.random.fold_in(jax.random.fold_in(splits[6], part), 71), part),
        "route_weights": jnp.clip(jnp.exp(math.log(1.0) - 2.3025851 * jax.random.uniform(own_keys[2], (TOKENS, TOP), jnp.float32) ** steps_of(own_keys[2], (TOKENS, TOP), ((0, 16),), -0.2, 0.2)), 0.1, 1.0),
        "w_gate": scatter_about(splits[3], (EXPERTS, D, FF), D ** -0.5, 0.078125, ((0, 2), (2, 8))),
        "w_up": scatter_about(splits[4], (EXPERTS, D, FF), D ** -0.5, 0.078125, ((0, 2), (2, 8))),
        "w_down": scatter_about(splits[5], (EXPERTS, FF, D), FF ** -0.5, 0.0625, ((0, 2), (1, 8))),
    }


def slots_of(expert_ids):
    choice_ids = expert_ids.reshape(-1, TOK_DEV * TOP)
    onehot = (choice_ids[..., None] == jnp.arange(EXPERTS, dtype=jnp.int32)).astype(jnp.int32)
    before = jnp.cumsum(onehot, axis=1) - onehot
    slot_index = jnp.sum(before * onehot, axis=-1)
    kept_mask = (jnp.sum(onehot, axis=-1) > 0) & (slot_index < CAP)
    return choice_ids, onehot, slot_index, kept_mask


def reference(tokens, expert_ids, route_weights, w_gate, w_up, w_down):
    block_count = TOKENS // TOK_DEV
    hidden_width = FF // N_EPT
    choice_ids, onehot, slot_index, kept_mask = slots_of(expert_ids)
    token_blocks = tokens.reshape(block_count, TOK_DEV, D)
    matches = (onehot.transpose(0, 2, 1)[:, :, None, :] == 1)
    matches = matches & (slot_index[:, None, None, :] == jnp.arange(CAP, dtype=jnp.int32)[None, None, :, None])
    matches = matches & kept_mask[:, None, None, :]
    positions = jnp.sum(jnp.where(matches, jnp.arange(TOK_DEV * TOP, dtype=jnp.int32), 0), axis=-1) // TOP
    present = jnp.any(matches, axis=-1)
    picked_rows = jax.vmap(lambda block, where_rows: block[where_rows])(token_blocks, positions.reshape(block_count, -1))
    dispatched = picked_rows.reshape(block_count, EXPERTS, CAP, D)
    dispatched = jnp.where(present[..., None], dispatched, jnp.zeros((), jnp.bfloat16))
    outputs = []
    for expert in range(EXPERTS):
        row_block = dispatched[:, expert].reshape(-1, D)
        gate_value = jnp.dot(row_block, w_gate[expert], preferred_element_type=jnp.float32)
        up_value = jnp.dot(row_block, w_up[expert], preferred_element_type=jnp.float32)
        hidden = (jax.nn.silu(gate_value) * up_value).astype(jnp.bfloat16)
        hidden_parts = hidden.reshape(-1, N_EPT, hidden_width).transpose(1, 0, 2)
        down_parts = w_down[expert].reshape(N_EPT, hidden_width, D)

        def add_part(running, operand):
            part_hidden, part_down = operand
            rounded = jnp.dot(part_hidden, part_down, preferred_element_type=jnp.float32).astype(jnp.bfloat16)
            rounded = lax.optimization_barrier(rounded)
            return running + rounded.astype(jnp.float32), None

        running, _ = lax.scan(add_part, jnp.zeros((row_block.shape[0], D), jnp.float32), (hidden_parts, down_parts))
        outputs.append(running.astype(jnp.bfloat16).reshape(block_count, CAP, D))
    expert_out = jnp.stack(outputs, axis=1).reshape(block_count, EXPERTS * CAP, D)
    row_index = jnp.where(kept_mask, jnp.clip(choice_ids * CAP + slot_index, 0, EXPERTS * CAP - 1), 0).astype(jnp.int32)
    picked = jax.vmap(lambda block, where_rows: block[where_rows])(expert_out, row_index).astype(jnp.float32)
    scaled = route_weights.reshape(block_count, -1) * kept_mask.astype(jnp.float32)
    mixed_out = jnp.sum((picked * scaled[..., None]).reshape(block_count, TOK_DEV, TOP, D), axis=2)
    return mixed_out.reshape(TOKENS, D).astype(jnp.bfloat16)
```

```python
import jax
import jax.numpy as jnp
from jax import lax
from jax.experimental import pallas as pl
from jax.experimental.pallas import tpu as pltpu
from jax.sharding import PartitionSpec as P

CAP = 16
BLOCK = 2 * CAP
LANES = 128
VMEM_LIMIT = 8 * 1024 * 1024


def ring_pairs(count, columns):
    rows = count // columns
    if columns == 2:
        cycle = [2 * r for r in range(rows)] + [2 * r + 1 for r in reversed(range(rows))]
    else:
        cycle = list(range(count))
    forward = [(cycle[i], cycle[(i + 1) % count]) for i in range(count)]
    return forward, [(b, a) for a, b in forward]


def swap(value):
    return lax.ppermute(value, "exp", [(0, 1), (1, 0)])


def tile_of(size, most):
    return max(t for t in range(LANES, most + 1, LANES) if size % t == 0)


def in_hbm(value):
    return pltpu.with_memory_space_constraint(value, pltpu.HBM)


def dispatch_kernel(me_ref, ids_ref, weights_ref, tokens_ref, mine_ref, theirs_ref, mixer_ref, picker):
    @pl.when(pl.program_id(0) == 0)
    def _():
        token_count = ids_ref.shape[1]
        line = lax.broadcasted_iota(jnp.int32, (BLOCK, token_count), 0)
        expert = (line // CAP + me_ref[0]) % 2
        first = ids_ref[0:1, :] == expert
        second = ids_ref[1:2, :] == expert
        named = first.astype(jnp.float32) + second.astype(jnp.float32)
        row = lax.broadcasted_iota(jnp.int32, (token_count, token_count), 0)
        column = lax.broadcasted_iota(jnp.int32, (token_count, token_count), 1)
        earlier = (row < column).astype(jnp.bfloat16)
        before = jnp.dot(named.astype(jnp.bfloat16), earlier, preferred_element_type=jnp.float32)
        slot = (line % CAP).astype(jnp.float32)
        hit_first = jnp.where(first & (before == slot), 1.0, 0.0)
        after = before + first.astype(jnp.float32)
        hit_second = jnp.where(second & (after == slot), 1.0, 0.0)
        picker[...] = (hit_first + hit_second).astype(jnp.bfloat16)
        mixer = hit_first * weights_ref[0:1, :] + hit_second * weights_ref[1:2, :]
        high = mixer.astype(jnp.bfloat16).astype(jnp.float32)
        empty = jnp.zeros((LANES - 2 * BLOCK, token_count), jnp.float32)
        stacked = jnp.concatenate([high, mixer - high, empty], axis=0)
        mixer_ref[...] = stacked.T.astype(jnp.bfloat16)

    rows = jnp.dot(picker[...], tokens_ref[...], preferred_element_type=jnp.float32)
    mine_ref[...] = rows[:CAP].astype(jnp.bfloat16)
    theirs_ref[...] = rows[CAP:].astype(jnp.bfloat16)


def dispatch(me, expert_ids, route_weights, tokens):
    token_count, width = tokens.shape
    tile = tile_of(width, 1536)
    whole = lambda j, me: (0, 0)
    column = lambda j, me: (0, j)
    return pl.pallas_call(
        dispatch_kernel,
        grid_spec=pltpu.PrefetchScalarGridSpec(
            num_scalar_prefetch=1,
            grid=(width // tile,),
            in_specs=[
                pl.BlockSpec((2, token_count), whole),
                pl.BlockSpec((2, token_count), whole),
                pl.BlockSpec((token_count, tile), column),
            ],
            out_specs=[
                pl.BlockSpec((CAP, tile), column),
                pl.BlockSpec((CAP, tile), column),
                pl.BlockSpec((token_count, LANES), whole),
            ],
            scratch_shapes=[pltpu.VMEM((BLOCK, token_count), jnp.bfloat16)],
        ),
        out_shape=[
            jax.ShapeDtypeStruct((CAP, width), jnp.bfloat16),
            jax.ShapeDtypeStruct((CAP, width), jnp.bfloat16),
            jax.ShapeDtypeStruct((token_count, LANES), jnp.bfloat16),
        ],
        compiler_params=pltpu.CompilerParams(vmem_limit_bytes=VMEM_LIMIT),
        name="dispatch",
    )(me, in_hbm(expert_ids.T), in_hbm(route_weights.T), in_hbm(tokens))


def hold_kernel(source_ref, held_ref, done):
    copy = pltpu.make_async_copy(source_ref, held_ref, done)
    copy.start()
    copy.wait()


def hold(weights):
    return pl.pallas_call(
        hold_kernel,
        in_specs=[pl.BlockSpec(memory_space=pltpu.HBM)],
        out_specs=pl.BlockSpec(memory_space=pltpu.VMEM),
        out_shape=pltpu.VMEM(weights.shape, weights.dtype),
        scratch_shapes=[pltpu.SemaphoreType.DMA],
        cost_estimate=pl.CostEstimate(
            flops=0, bytes_accessed=2 * weights.size, transcendentals=0
        ),
        compiler_params=pltpu.CompilerParams(vmem_limit_bytes=VMEM_LIMIT),
        name="hold",
    )(in_hbm(weights))


def hidden_kernel(count, *refs):
    rows, (gate_ref, up_ref, out_ref) = refs[:count], refs[count:]
    block = jnp.concatenate([r[...] for r in rows], axis=0)
    width = out_ref.shape[1]
    tile = tile_of(width, 256)

    @pl.loop(0, width // tile)
    def _(j):
        here = pl.ds(pl.multiple_of(j * tile, tile), tile)
        gate = jnp.dot(block, gate_ref[:, here], preferred_element_type=jnp.float32)
        up = jnp.dot(block, up_ref[:, here], preferred_element_type=jnp.float32)
        out_ref[:, here] = (gate / (1.0 + jnp.exp(-gate)) * up).astype(jnp.bfloat16)


def hidden_of(rows, w_gate, w_up):
    depth, width = w_gate.shape
    total = sum(r.shape[0] for r in rows)
    local = pl.BlockSpec(memory_space=pltpu.VMEM)
    return pl.pallas_call(
        lambda *refs: hidden_kernel(len(rows), *refs),
        in_specs=[local] * (len(rows) + 2),
        out_specs=local,
        out_shape=jax.ShapeDtypeStruct((total, width), jnp.bfloat16),
        cost_estimate=pl.CostEstimate(
            flops=4 * total * depth * width,
            bytes_accessed=4 * depth * width,
            transcendentals=total * width,
        ),
        compiler_params=pltpu.CompilerParams(vmem_limit_bytes=VMEM_LIMIT),
        name="hidden",
    )(*rows, w_gate, w_up)


def product_kernel(start, count, hidden_ref, down_ref, out_ref):
    width = out_ref.shape[1]
    tile = tile_of(width, 512)
    block = hidden_ref[start : start + count, :]

    @pl.loop(0, width // tile)
    def _(j):
        here = pl.ds(pl.multiple_of(j * tile, tile), tile)
        out_ref[:, here] = jnp.dot(
            block, down_ref[:, here], preferred_element_type=jnp.float32
        ).astype(jnp.bfloat16)


def product_of(hidden, start, count, w_down):
    depth, width = w_down.shape
    local = pl.BlockSpec(memory_space=pltpu.VMEM)
    return pl.pallas_call(
        lambda *refs: product_kernel(start, count, *refs),
        in_specs=[local, local],
        out_specs=local,
        out_shape=jax.ShapeDtypeStruct((count, width), jnp.bfloat16),
        cost_estimate=pl.CostEstimate(
            flops=2 * count * depth * width, bytes_accessed=2 * depth * width, transcendentals=0
        ),
        compiler_params=pltpu.CompilerParams(vmem_limit_bytes=VMEM_LIMIT),
        name="product",
    )(hidden, pltpu.with_memory_space_constraint(w_down, pltpu.VMEM))


def combine_kernel(own_ref, ahead_ref, behind_ref, theirs_ref, mixer_ref, out_ref):
    mine = (
        own_ref[...].astype(jnp.float32)
        + ahead_ref[...].astype(jnp.float32)
        + behind_ref[...].astype(jnp.float32)
    ).astype(jnp.bfloat16)
    theirs = theirs_ref[...]
    rows = jnp.concatenate([mine, theirs, mine, theirs], axis=0)
    out_ref[...] = jnp.dot(
        mixer_ref[:, : 2 * BLOCK], rows, preferred_element_type=jnp.float32
    ).astype(jnp.bfloat16)


def combine(own, ahead, behind, theirs, mixer):
    width = own.shape[1]
    token_count = mixer.shape[0]
    tile = tile_of(width, 1536)
    part = pl.BlockSpec((CAP, tile), lambda j: (0, j))
    return pl.pallas_call(
        combine_kernel,
        grid=(width // tile,),
        in_specs=[part, part, part, part, pl.BlockSpec(mixer.shape, lambda j: (0, 0))],
        out_specs=pl.BlockSpec((token_count, tile), lambda j: (0, j)),
        out_shape=jax.ShapeDtypeStruct((token_count, width), jnp.bfloat16),
        compiler_params=pltpu.CompilerParams(vmem_limit_bytes=VMEM_LIMIT),
        name="combine",
    )(own, ahead, behind, theirs, mixer)


def body(tokens, expert_ids, route_weights, w_gate, w_up, w_down):
    ept_count = lax.axis_size("ept")
    forward, backward = ring_pairs(ept_count, 2 if ept_count == 8 else 1)
    reach = ept_count // 2
    half = tokens.shape[1] // 2
    w_gate, w_up, w_down = w_gate[0], w_up[0], w_down[0]
    me = lax.axis_index("exp").astype(jnp.int32).reshape(1)
    mine, theirs, mixer = dispatch(me, expert_ids, route_weights, tokens)
    own = jnp.concatenate([mine, swap(theirs)], axis=0)

    ahead = behind = own
    arrived = [(own,)]
    held = []
    for k in range(1, reach):
        if k > 1 and len(held) < 2:
            weights = hold((w_gate, w_up)[len(held)])
            ahead, behind, weights = lax.optimization_barrier((ahead, behind, weights))
            held.append(pltpu.with_memory_space_constraint(weights, pltpu.VMEM))
        ahead = lax.ppermute(ahead, "ept", forward)
        behind = lax.ppermute(behind, "ept", backward)
        arrived.append((behind, ahead))
    w_gate, w_up = held
    early = [r for k in range(reach - 1) for r in arrived[reach - 2 - k]]
    hidden_early = hidden_of(early, w_gate, w_up)
    ahead, behind, w_down, hidden_early = lax.optimization_barrier((ahead, behind, w_down, hidden_early))
    ahead = lax.ppermute(ahead[:, :half], "ept", forward)
    behind = lax.ppermute(behind[:, half:], "ept", backward)
    w_down = hold(w_down)
    arrived.append((jnp.concatenate([ahead, behind], axis=1),))
    late = [r for k in (reach - 1, reach) for r in arrived[k]]
    hidden_late = hidden_of(late, w_gate, w_up)

    def product_at(k):
        if k == reach:
            return product_of(hidden_late, 2 * BLOCK, BLOCK, w_down)
        if k == reach - 1:
            return product_of(hidden_late, 0, 2 * BLOCK, w_down)
        return product_of(
            hidden_early, 2 * BLOCK * (reach - 2 - k), 2 * BLOCK if k else BLOCK, w_down
        )

    product = product_at(reach)
    ahead = lax.ppermute(product[:, :half], "ept", forward)
    behind = lax.ppermute(product[:, half:], "ept", backward)
    for k in reversed(range(1, reach)):
        product = product_at(k)
        to_ahead, to_behind = product[:BLOCK], product[BLOCK:]
        if k == reach - 1:
            to_ahead = jnp.concatenate([to_ahead[:, :half] + ahead, to_ahead[:, half:]], axis=1)
            to_behind = jnp.concatenate([to_behind[:, :half], to_behind[:, half:] + behind], axis=1)
        else:
            to_ahead += ahead
            to_behind += behind
        ahead = lax.ppermute(to_ahead, "ept", forward)
        behind = lax.ppermute(to_behind, "ept", backward)
    product = product_at(0)
    for_theirs = (
        product[CAP:].astype(jnp.float32)
        + ahead[CAP:].astype(jnp.float32)
        + behind[CAP:].astype(jnp.float32)
    ).astype(jnp.bfloat16)
    return combine(product, ahead, behind, swap(for_theirs), mixer)


def solution(mesh):
    placed = (
        P(("groups", "ept", "exp"), None),
        P(("groups", "ept", "exp"), None),
        P(("groups", "ept", "exp"), None),
        P("exp", None, "ept"),
        P("exp", None, "ept"),
        P("exp", "ept", None),
    )
    return jax.shard_map(
        body,
        mesh=mesh,
        in_specs=placed,
        out_specs=P(("groups", "ept", "exp"), None),
        check_vma=False,
    )
```

```python
import jax
import jax.numpy as jnp
from jax import lax
from jax.experimental import pallas as pl
from jax.experimental.pallas import tpu as pltpu
from jax.sharding import PartitionSpec as P

CAP = 16
BLOCK = 2 * CAP
LANES = 128
ROWS = 256
VMEM_LIMIT = 8 * 1024 * 1024


def ring_hops(count, cores):
    cycle = [0, 2, 4, 6, 7, 5, 3, 1] if count == 8 else list(range(count))
    hops = []
    for here, there in zip(cycle, cycle[1:] + cycle[:1]):
        hops.append((here * cores, there * cores))
        hops.append((there * cores + 1, here * cores + 1))
    return hops


def swap(value):
    return lax.ppermute(value, "exp", [(0, 1), (1, 0)])


def tile_of(size, most):
    return max(t for t in range(LANES, most + 1, LANES) if size % t == 0)


def in_hbm(value):
    return pltpu.with_memory_space_constraint(value, pltpu.HBM)


def dispatch_kernel(me_ref, ids_ref, weights_ref, tokens_ref, rows_ref, turned_ref, mixer_ref, picker):
    @pl.when(pl.program_id(0) == 0)
    def _():
        token_count = ids_ref.shape[1]
        line = lax.broadcasted_iota(jnp.int32, (BLOCK, token_count), 0)
        expert = (line // CAP + me_ref[0]) % 2
        first = ids_ref[0:1, :] == expert
        second = ids_ref[1:2, :] == expert
        named = first.astype(jnp.float32) + second.astype(jnp.float32)
        row = lax.broadcasted_iota(jnp.int32, (token_count, token_count), 0)
        column = lax.broadcasted_iota(jnp.int32, (token_count, token_count), 1)
        earlier = (row < column).astype(jnp.bfloat16)
        before = jnp.dot(named.astype(jnp.bfloat16), earlier, preferred_element_type=jnp.float32)
        slot = (line % CAP).astype(jnp.float32)
        hit_first = jnp.where(first & (before == slot), 1.0, 0.0)
        after = before + first.astype(jnp.float32)
        hit_second = jnp.where(second & (after == slot), 1.0, 0.0)
        picker[...] = (hit_first + hit_second).astype(jnp.bfloat16)
        mixer = hit_first * weights_ref[0:1, :] + hit_second * weights_ref[1:2, :]
        high = mixer.astype(jnp.bfloat16).astype(jnp.float32)
        empty = jnp.zeros((LANES - 2 * BLOCK, token_count), jnp.float32)
        stacked = jnp.concatenate([high, mixer - high, empty], axis=0)
        mixer_ref[...] = stacked.T.astype(jnp.bfloat16)

    rows = jnp.dot(picker[...], tokens_ref[...], preferred_element_type=jnp.float32)
    rows_ref[...] = rows.astype(jnp.bfloat16)
    turned_ref[:CAP, :] = rows[CAP:].astype(jnp.bfloat16)
    turned_ref[CAP:, :] = rows[:CAP].astype(jnp.bfloat16)


def dispatch(me, expert_ids, route_weights, tokens):
    token_count, width = tokens.shape
    tile = tile_of(width, 1536)
    whole = lambda j, me: (0, 0)
    column = lambda j, me: (0, j)
    return pl.pallas_call(
        dispatch_kernel,
        grid_spec=pltpu.PrefetchScalarGridSpec(
            num_scalar_prefetch=1,
            grid=(width // tile,),
            in_specs=[
                pl.BlockSpec((2, token_count), whole),
                pl.BlockSpec((2, token_count), whole),
                pl.BlockSpec((token_count, tile), column),
            ],
            out_specs=[
                pl.BlockSpec((BLOCK, tile), column),
                pl.BlockSpec((BLOCK, tile), column),
                pl.BlockSpec((token_count, LANES), whole),
            ],
            scratch_shapes=[pltpu.VMEM((BLOCK, token_count), jnp.bfloat16)],
        ),
        out_shape=[
            jax.ShapeDtypeStruct((BLOCK, width), jnp.bfloat16),
            jax.ShapeDtypeStruct((BLOCK, width), jnp.bfloat16),
            jax.ShapeDtypeStruct((token_count, LANES), jnp.bfloat16),
        ],
        compiler_params=pltpu.CompilerParams(vmem_limit_bytes=VMEM_LIMIT),
        name="dispatch",
    )(me, in_hbm(expert_ids.T), in_hbm(route_weights.T), in_hbm(tokens))


def call(kernel, name, operands, outs, scratch=(), flops=0, bytes_accessed=0):
    return pl.pallas_call(
        kernel,
        in_specs=[pl.BlockSpec(memory_space=m) for _, m in operands],
        out_specs=[pl.BlockSpec(memory_space=pltpu.VMEM)] * len(outs),
        out_shape=outs,
        scratch_shapes=scratch,
        cost_estimate=pl.CostEstimate(
            flops=flops, bytes_accessed=bytes_accessed, transcendentals=0
        ),
        compiler_params=pltpu.CompilerParams(vmem_limit_bytes=VMEM_LIMIT),
        name=name,
    )(*[v for v, _ in operands])


def local(*values):
    return [(v, pltpu.VMEM) for v in values]


def held(*values):
    return [(pltpu.with_memory_space_constraint(v, pltpu.VMEM), pltpu.VMEM) for v in values]


def remote(*values):
    return [(in_hbm(v), pltpu.HBM) for v in values]


def array(*shape, dtype=jnp.bfloat16):
    return jax.ShapeDtypeStruct(shape, dtype)


def activate(gate, up):
    return (gate / (1.0 + jnp.exp(-gate)) * up).astype(jnp.bfloat16)


def hold_and_multiply(rows, weights, begin, depth, before, pieces=4):
    width = weights.shape[1]
    total = sum(c for _, _, c in rows)
    step = depth // pieces
    before = [] if before is None else [before]

    def kernel(*refs):
        row_refs, (source_ref, *refs) = refs[: len(rows)], refs[len(rows) :]
        held_ref, sum_ref, done = refs[len(before) :]
        copies = [
            pltpu.make_async_copy(
                source_ref.at[pl.ds(begin + i * step, step)],
                held_ref.at[pl.ds(i * step, step)],
                done.at[i],
            )
            for i in range(pieces)
        ]
        for copy in copies:
            copy.start()
        for i, copy in enumerate(copies):
            there = slice(begin + i * step, begin + (i + 1) * step)
            block = jnp.concatenate(
                [r[f : f + c, there] for r, (_, f, c) in zip(row_refs, rows)], axis=0
            )
            copy.wait()
            value = jnp.dot(
                block, held_ref[i * step : (i + 1) * step, :], preferred_element_type=jnp.float32
            )
            if i:
                value += sum_ref[...]
            elif before:
                value += refs[0][...]
            sum_ref[...] = value

    return call(
        kernel,
        "hold_and_multiply",
        local(*[r for r, _, _ in rows]) + remote(weights) + local(*before),
        [pltpu.VMEM((depth, width), weights.dtype), array(total, width, dtype=jnp.float32)],
        [pltpu.SemaphoreType.DMA((pieces,))],
        flops=2 * total * depth * width,
        bytes_accessed=2 * depth * width,
    )


def hidden_of(rows, gates, ups, gate_done=None, up_done=None):
    total = sum(c for _, _, c in rows)
    width = gates[0].shape[1]
    tile = tile_of(width, 256)
    before = [] if gate_done is None else [gate_done, up_done]

    def kernel(*refs):
        row_refs, refs = refs[: len(rows)], refs[len(rows) :]
        gate_refs, refs = refs[: len(gates)], refs[len(gates) :]
        up_refs, (*before_refs, out_ref) = refs[: len(ups)], refs[len(ups) :]
        block = jnp.concatenate([r[f : f + c, :] for r, (_, f, c) in zip(row_refs, rows)], axis=0)

        @pl.loop(0, width // tile)
        def _(j):
            here = pl.ds(pl.multiple_of(j * tile, tile), tile)
            values = []
            for i, pieces in enumerate((gate_refs, up_refs)):
                known = before_refs[i].shape[0] if before_refs else 0
                value, first = 0.0, 0
                for ref in pieces:
                    last = first + ref.shape[0]
                    value += jnp.dot(
                        block[known:, first:last], ref[:, here], preferred_element_type=jnp.float32
                    )
                    first = last
                if known:
                    value = jnp.concatenate([before_refs[i][:, here], value], axis=0)
                values.append(value)
            out_ref[:, here] = activate(*values)

    depth = sum(g.shape[0] for g in gates)
    return call(
        kernel,
        "hidden",
        local(*[r for r, _, _ in rows]) + held(*gates, *ups) + local(*before),
        [array(total, width)],
        flops=4 * total * depth * width,
        bytes_accessed=4 * depth * width,
    )[0]


def add(value, *others):
    total = value.astype(jnp.float32)
    for other in others:
        total += other.astype(jnp.float32)
    return total.astype(jnp.bfloat16)


def combine(arrived, handed, product, mixer):
    width = arrived.shape[1]
    token_count = mixer.shape[0]
    tile = tile_of(width, 1536)
    column = lambda j: (0, j)

    def kernel(arrived_ref, handed_ref, product_ref, mixer_ref, out_ref):
        rows = arrived_ref[...].astype(jnp.float32) + handed_ref[...].astype(jnp.float32)
        mine = (rows[:CAP] + product_ref[...].astype(jnp.float32)).astype(jnp.bfloat16)
        theirs = rows[CAP:].astype(jnp.bfloat16)
        rows = jnp.concatenate([mine, theirs, mine, theirs], axis=0)
        out_ref[...] = jnp.dot(
            mixer_ref[:, : 2 * BLOCK], rows, preferred_element_type=jnp.float32
        ).astype(jnp.bfloat16)

    return pl.pallas_call(
        kernel,
        grid=(width // tile,),
        in_specs=[
            pl.BlockSpec((BLOCK, tile), column),
            pl.BlockSpec((BLOCK, tile), column),
            pl.BlockSpec((CAP, tile), column),
            pl.BlockSpec(mixer.shape, lambda j: (0, 0)),
        ],
        out_specs=pl.BlockSpec((token_count, tile), column),
        out_shape=array(token_count, width),
        compiler_params=pltpu.CompilerParams(vmem_limit_bytes=VMEM_LIMIT),
        name="combine",
    )(arrived, handed, product, mixer)


def after(value, other):
    return lax.optimization_barrier((value, other))


def body(tokens, expert_ids, route_weights, w_gate, w_up, w_down):
    ept_count = lax.axis_size("ept")
    hops = ring_hops(ept_count, lax.axis_size("exp"))
    reach = ept_count // 2
    w_gate, w_up, w_down = w_gate[0], w_up[0], w_down[0]
    me = lax.axis_index("exp").astype(jnp.int32).reshape(1)

    def hop(value):
        return lax.ppermute(value, ("ept", "exp"), hops)

    own, turned, mixer = dispatch(me, expert_ids, route_weights, tokens)
    units = [own, swap(turned)]
    arriving = [hop(units[0]), hop(units[1])]
    plan = [(0, 0, 1, 3, 4, 5), (1, 0, 1, 5, 6, 8)] if ept_count == 8 else []
    weights, held_weights, sums, todo = [w_up, w_gate], [[], []], [None, None], []
    given = [None]
    while len(units) < 2 * reach + 1:
        unit = arriving[len(units) - 2]
        for i, before in list(todo):
            if before == len(units):
                unit, sums[i] = after(unit, sums[i])
                todo.remove((i, before))
        units.append(unit)
        if len(arriving) < 2 * reach - 1:
            arriving.append(hop(unit))
        for i, part, parts, newest, count, before in plan:
            if newest == len(units) - 1:
                units[-1], source = after(units[-1], weights[i])
                depth = source.shape[0] // parts
                rows = [(u, 0, CAP) for u in units[:count]]
                if given[-1] is not None and i == 1 and part == 0:
                    source, given[-1] = after(source, given[-1])
                piece, sums[i] = hold_and_multiply(rows, source, part * depth, depth, sums[i])
                held_weights[i].append(piece)
                todo.append((i, before))
        if len(units) == 2 * reach - 2:
            given = [swap(jnp.concatenate([u[CAP:] for u in units[2:]], axis=0))]
    far = swap(jnp.concatenate([u[CAP:] for u in units[-3:]], axis=0))
    ups, gates = (h if h else [w] for h, w in zip(held_weights, weights))
    up_done, gate_done = sums

    rows = [(u, 0, CAP) for u in units[:-1]]
    rows += [(given[0], BLOCK * k, BLOCK) for k in range(reach - 2)] + [(far, 0, BLOCK)]
    rows += [(units[-1], 0, CAP), (far, BLOCK, CAP)]
    groups = [[]]
    for row in rows:
        if sum(c for _, _, c in groups[-1]) + row[2] > ROWS:
            groups.append([])
        groups[-1].append(row)
    hidden = [hidden_of(groups[0], gates, ups, gate_done, up_done)]
    hidden += [hidden_of(group, gates, ups) for group in groups[1:]]
    hidden = jnp.concatenate(hidden, axis=0) if len(hidden) > 1 else hidden[0]
    mine = [hidden[BLOCK * k : BLOCK * (k + 1)] for k in range(reach)]
    others = [hidden[BLOCK * k : BLOCK * (k + 1)] for k in range(reach, 2 * reach)]

    def product_of(*parts):
        product = jnp.dot(
            jnp.concatenate(parts, axis=0), w_down, preferred_element_type=jnp.float32
        )
        return lax.optimization_barrier(product.astype(jnp.bfloat16))

    product = product_of(mine[reach - 1], *others[-2:])
    handed, kept = [swap(product[:BLOCK])], [product[BLOCK : 2 * BLOCK]]
    a = product[2 * BLOCK :]
    a = hop(jnp.concatenate([a[:CAP], swap(a[CAP:])], axis=0))
    product = product_of(*mine[:-1], *others[:-2])
    own = product[:BLOCK]
    if reach > 2:
        more = swap(product[BLOCK : BLOCK * (reach - 1)])
        handed += [more[BLOCK * k : BLOCK * (k + 1)] for k in reversed(range(reach - 2))]
        more = product[BLOCK * (reach - 1) :]
        kept += [more[BLOCK * k : BLOCK * (k + 1)] for k in reversed(range(reach - 2))]
    b = None
    for mine, theirs in zip(kept, handed):
        unit = jnp.concatenate([mine[:CAP], theirs[:CAP]], axis=0)
        b = hop(unit if b is None else add(unit, b))
        a = hop(add(jnp.concatenate([mine[CAP:], theirs[CAP:]], axis=0), a))
    handover = swap(jnp.concatenate([b[CAP:], add(b[:CAP], own[CAP:])], axis=0))
    return combine(a, handover, own[:CAP], mixer)


def solution(mesh):
    placed = (
        P(("groups", "ept", "exp"), None),
        P(("groups", "ept", "exp"), None),
        P(("groups", "ept", "exp"), None),
        P("exp", None, "ept"),
        P("exp", None, "ept"),
        P("exp", "ept", None),
    )
    return jax.shard_map(
        body,
        mesh=mesh,
        in_specs=placed,
        out_specs=P(("groups", "ept", "exp"), None),
        check_vma=False,
    )
```

```python
import jax
import jax.numpy as jnp
from jax import lax
from jax.experimental import pallas as pl
from jax.experimental.pallas import tpu as pltpu
from jax.sharding import PartitionSpec as P

CAP = 16
BLOCK = 2 * CAP
LANES = 128
ROWS = 256
VMEM_LIMIT = 8 * 1024 * 1024


def ring_hops(count, cores):
    cycle = [0, 2, 4, 6, 7, 5, 3, 1] if count == 8 else list(range(count))
    hops = []
    for here, there in zip(cycle, cycle[1:] + cycle[:1]):
        hops.append((here * cores, there * cores))
        hops.append((there * cores + 1, here * cores + 1))
    return hops


def swap(value):
    return lax.ppermute(value, "exp", [(0, 1), (1, 0)])


def tile_of(size, most):
    return max(t for t in range(LANES, most + 1, LANES) if size % t == 0)


def in_hbm(value):
    return pltpu.with_memory_space_constraint(value, pltpu.HBM)


def dispatch_kernel(me_ref, ids_ref, weights_ref, tokens_ref, rows_ref, turned_ref, mixer_ref, picker):
    @pl.when(pl.program_id(0) == 0)
    def _():
        token_count = ids_ref.shape[1]
        line = lax.broadcasted_iota(jnp.int32, (BLOCK, token_count), 0)
        expert = (line // CAP + me_ref[0]) % 2
        first = ids_ref[0:1, :] == expert
        second = ids_ref[1:2, :] == expert
        named = first.astype(jnp.float32) + second.astype(jnp.float32)
        row = lax.broadcasted_iota(jnp.int32, (token_count, token_count), 0)
        column = lax.broadcasted_iota(jnp.int32, (token_count, token_count), 1)
        earlier = (row < column).astype(jnp.bfloat16)
        before = jnp.dot(named.astype(jnp.bfloat16), earlier, preferred_element_type=jnp.float32)
        slot = (line % CAP).astype(jnp.float32)
        hit_first = jnp.where(first & (before == slot), 1.0, 0.0)
        after = before + first.astype(jnp.float32)
        hit_second = jnp.where(second & (after == slot), 1.0, 0.0)
        picker[...] = (hit_first + hit_second).astype(jnp.bfloat16)
        mixer = hit_first * weights_ref[0:1, :] + hit_second * weights_ref[1:2, :]
        high = mixer.astype(jnp.bfloat16).astype(jnp.float32)
        empty = jnp.zeros((LANES - 2 * BLOCK, token_count), jnp.float32)
        stacked = jnp.concatenate([high, mixer - high, empty], axis=0)
        mixer_ref[...] = stacked.T.astype(jnp.bfloat16)

    rows = jnp.dot(picker[...], tokens_ref[...], preferred_element_type=jnp.float32)
    rows_ref[...] = rows.astype(jnp.bfloat16)
    turned_ref[:CAP, :] = rows[CAP:].astype(jnp.bfloat16)
    turned_ref[CAP:, :] = rows[:CAP].astype(jnp.bfloat16)


def dispatch(me, expert_ids, route_weights, tokens):
    token_count, width = tokens.shape
    tile = tile_of(width, 3072)
    whole = lambda j, me: (0, 0)
    column = lambda j, me: (0, j)
    return pl.pallas_call(
        dispatch_kernel,
        grid_spec=pltpu.PrefetchScalarGridSpec(
            num_scalar_prefetch=1,
            grid=(width // tile,),
            in_specs=[
                pl.BlockSpec((2, token_count), whole),
                pl.BlockSpec((2, token_count), whole),
                pl.BlockSpec((token_count, tile), column),
            ],
            out_specs=[
                pl.BlockSpec((BLOCK, tile), column),
                pl.BlockSpec((BLOCK, tile), column),
                pl.BlockSpec((token_count, LANES), whole),
            ],
            scratch_shapes=[pltpu.VMEM((BLOCK, token_count), jnp.bfloat16)],
        ),
        out_shape=[
            jax.ShapeDtypeStruct((BLOCK, width), jnp.bfloat16),
            jax.ShapeDtypeStruct((BLOCK, width), jnp.bfloat16),
            jax.ShapeDtypeStruct((token_count, LANES), jnp.bfloat16),
        ],
        compiler_params=pltpu.CompilerParams(vmem_limit_bytes=VMEM_LIMIT),
        name="dispatch",
    )(me, in_hbm(expert_ids.T), in_hbm(route_weights.T), in_hbm(tokens))


def call(kernel, name, operands, outs, scratch=(), flops=0, bytes_accessed=0):
    return pl.pallas_call(
        kernel,
        in_specs=[pl.BlockSpec(memory_space=m) for _, m in operands],
        out_specs=[pl.BlockSpec(memory_space=pltpu.VMEM)] * len(outs),
        out_shape=outs,
        scratch_shapes=scratch,
        cost_estimate=pl.CostEstimate(
            flops=flops, bytes_accessed=bytes_accessed, transcendentals=0
        ),
        compiler_params=pltpu.CompilerParams(vmem_limit_bytes=VMEM_LIMIT),
        name=name,
    )(*[v for v, _ in operands])


def local(*values):
    return [(v, pltpu.VMEM) for v in values]


def held(*values):
    return [(pltpu.with_memory_space_constraint(v, pltpu.VMEM), pltpu.VMEM) for v in values]


def remote(*values):
    return [(in_hbm(v), pltpu.HBM) for v in values]


def array(*shape, dtype=jnp.bfloat16):
    return jax.ShapeDtypeStruct(shape, dtype)


def activate(gate, up):
    return (gate / (1.0 + jnp.exp(-gate)) * up).astype(jnp.bfloat16)


def hold_and_multiply(rows, weights, begin, depth, before):
    width = weights.shape[1]
    total = sum(c for _, _, c in rows)
    step = tile_of(depth, 1536)
    pieces = depth // step
    before = [] if before is None else [before]

    def kernel(*refs):
        row_refs, (source_ref, *refs) = refs[: len(rows)], refs[len(rows) :]
        held_ref, sum_ref, done = refs[len(before) :]
        copies = [
            pltpu.make_async_copy(
                source_ref.at[pl.ds(begin + i * step, step)],
                held_ref.at[pl.ds(i * step, step)],
                done.at[i],
            )
            for i in range(pieces)
        ]
        for copy in copies:
            copy.start()
        for i, copy in enumerate(copies):
            there = slice(begin + i * step, begin + (i + 1) * step)
            block = jnp.concatenate(
                [r[f : f + c, there] for r, (_, f, c) in zip(row_refs, rows)], axis=0
            )
            copy.wait()
            value = jnp.dot(
                block, held_ref[i * step : (i + 1) * step, :], preferred_element_type=jnp.float32
            )
            if i:
                value += sum_ref[...]
            elif before:
                value += refs[0][...]
            sum_ref[...] = value

    return call(
        kernel,
        "hold_and_multiply",
        local(*[r for r, _, _ in rows]) + remote(weights) + local(*before),
        [pltpu.VMEM((depth, width), weights.dtype), array(total, width, dtype=jnp.float32)],
        [pltpu.SemaphoreType.DMA((pieces,))],
        flops=2 * total * depth * width,
        bytes_accessed=2 * depth * width,
    )


def hidden_of(rows, gates, ups, gate_done=None, up_done=None):
    total = sum(c for _, _, c in rows)
    width = gates[0].shape[1]
    tile = tile_of(width, 256)
    before = [] if gate_done is None else [gate_done, up_done]

    def kernel(*refs):
        row_refs, refs = refs[: len(rows)], refs[len(rows) :]
        gate_refs, refs = refs[: len(gates)], refs[len(gates) :]
        up_refs, (*before_refs, out_ref) = refs[: len(ups)], refs[len(ups) :]
        block = jnp.concatenate([r[f : f + c, :] for r, (_, f, c) in zip(row_refs, rows)], axis=0)

        @pl.loop(0, width // tile)
        def _(j):
            here = pl.ds(pl.multiple_of(j * tile, tile), tile)
            values = []
            for i, pieces in enumerate((gate_refs, up_refs)):
                known = before_refs[i].shape[0] if before_refs else 0
                value, first = 0.0, 0
                for ref in pieces:
                    last = first + ref.shape[0]
                    value += jnp.dot(
                        block[known:, first:last], ref[:, here], preferred_element_type=jnp.float32
                    )
                    first = last
                if known:
                    value = jnp.concatenate([before_refs[i][:, here], value], axis=0)
                values.append(value)
            out_ref[:, here] = activate(*values)

    depth = sum(g.shape[0] for g in gates)
    return call(
        kernel,
        "hidden",
        local(*[r for r, _, _ in rows]) + held(*gates, *ups) + local(*before),
        [array(total, width)],
        flops=4 * total * depth * width,
        bytes_accessed=4 * depth * width,
    )[0]


def add(value, *others):
    total = value.astype(jnp.float32)
    for other in others:
        total += other.astype(jnp.float32)
    return total.astype(jnp.bfloat16)


def combine(arrived, handed, product, mixer):
    width = arrived.shape[1]
    token_count = mixer.shape[0]
    tile = tile_of(width, 3072)
    column = lambda j: (0, j)

    def kernel(arrived_ref, handed_ref, product_ref, mixer_ref, out_ref):
        rows = arrived_ref[...].astype(jnp.float32) + handed_ref[...].astype(jnp.float32)
        mine = (rows[:CAP] + product_ref[...].astype(jnp.float32)).astype(jnp.bfloat16)
        theirs = rows[CAP:].astype(jnp.bfloat16)
        rows = jnp.concatenate([mine, theirs, mine, theirs], axis=0)
        out_ref[...] = jnp.dot(
            mixer_ref[:, : 2 * BLOCK], rows, preferred_element_type=jnp.float32
        ).astype(jnp.bfloat16)

    return pl.pallas_call(
        kernel,
        grid=(width // tile,),
        in_specs=[
            pl.BlockSpec((BLOCK, tile), column),
            pl.BlockSpec((BLOCK, tile), column),
            pl.BlockSpec((CAP, tile), column),
            pl.BlockSpec(mixer.shape, lambda j: (0, 0)),
        ],
        out_specs=pl.BlockSpec((token_count, tile), column),
        out_shape=array(token_count, width),
        compiler_params=pltpu.CompilerParams(vmem_limit_bytes=VMEM_LIMIT),
        name="combine",
    )(arrived, handed, product, mixer)


def after(value, other):
    return lax.optimization_barrier((value, other))


def body(tokens, expert_ids, route_weights, w_gate, w_up, w_down):
    ept_count = lax.axis_size("ept")
    hops = ring_hops(ept_count, lax.axis_size("exp"))
    reach = ept_count // 2
    w_gate, w_up, w_down = w_gate[0], w_up[0], w_down[0]
    me = lax.axis_index("exp").astype(jnp.int32).reshape(1)

    def hop(value):
        return lax.ppermute(value, ("ept", "exp"), hops)

    own, turned, mixer = dispatch(me, expert_ids, route_weights, tokens)
    units = [own, swap(turned)]
    arriving = [hop(units[0]), hop(units[1])]
    plan = [(0, 0, 4, 2, 3, 3), (0, 4, 8, 3, 3, 5), (1, 0, 8, 5, 6, 8)] if ept_count == 8 else []
    weights, held_weights, sums, todo = [w_up, w_gate], [[], []], [None, None], []
    given = [None]
    while len(units) < 2 * reach + 1:
        unit = arriving[len(units) - 2]
        for i, before in list(todo):
            if before == len(units):
                unit, sums[i] = after(unit, sums[i])
                todo.remove((i, before))
        units.append(unit)
        if len(arriving) < 2 * reach - 1:
            arriving.append(hop(unit))
        for i, first, last, newest, count, before in plan:
            if newest == len(units) - 1:
                units[-1], source = after(units[-1], weights[i])
                eighth = source.shape[0] // 8
                rows = [(u, 0, CAP) for u in units[:count]]
                if given[-1] is not None and i == 1:
                    source, given[-1] = after(source, given[-1])
                piece, sums[i] = hold_and_multiply(
                    rows, source, first * eighth, (last - first) * eighth, sums[i]
                )
                held_weights[i].append(piece)
                todo.append((i, before))
        if len(units) == 2 * reach - 2:
            given = [swap(jnp.concatenate([u[CAP:] for u in units[2:]], axis=0))]
    far = swap(jnp.concatenate([u[CAP:] for u in units[-3:]], axis=0))
    ups, gates = (h if h else [w] for h, w in zip(held_weights, weights))
    up_done, gate_done = sums

    rows = [(u, 0, CAP) for u in units[:-1]]
    rows += [(given[0], BLOCK * k, BLOCK) for k in range(reach - 2)] + [(far, 0, BLOCK)]
    rows += [(units[-1], 0, CAP), (far, BLOCK, CAP)]
    groups = [[]]
    for row in rows:
        if sum(c for _, _, c in groups[-1]) + row[2] > ROWS:
            groups.append([])
        groups[-1].append(row)
    hidden = [hidden_of(groups[0], gates, ups, gate_done, up_done)]
    hidden += [hidden_of(group, gates, ups) for group in groups[1:]]
    hidden = jnp.concatenate(hidden, axis=0) if len(hidden) > 1 else hidden[0]
    mine = [hidden[BLOCK * k : BLOCK * (k + 1)] for k in range(reach)]
    others = [hidden[BLOCK * k : BLOCK * (k + 1)] for k in range(reach, 2 * reach)]

    def product_of(*parts):
        product = jnp.dot(
            jnp.concatenate(parts, axis=0), w_down, preferred_element_type=jnp.float32
        )
        return lax.optimization_barrier(product.astype(jnp.bfloat16))

    product = product_of(mine[reach - 1], *others[-2:])
    handed, kept = [swap(product[:BLOCK])], [product[BLOCK : 2 * BLOCK]]
    a = product[2 * BLOCK :]
    a = hop(jnp.concatenate([a[:CAP], swap(a[CAP:])], axis=0))
    first = jnp.concatenate([kept[0][:CAP], handed[0][:CAP]], axis=0)
    first, parts = after(first, (*mine[:-1], *others[:-2]))
    product = product_of(*parts)
    own = product[:BLOCK]
    if reach > 2:
        more = swap(product[BLOCK : BLOCK * (reach - 1)])
        handed += [more[BLOCK * k : BLOCK * (k + 1)] for k in reversed(range(reach - 2))]
        more = product[BLOCK * (reach - 1) :]
        kept += [more[BLOCK * k : BLOCK * (k + 1)] for k in reversed(range(reach - 2))]
    b = None
    for mine, theirs in zip(kept, handed):
        unit = jnp.concatenate([mine[:CAP], theirs[:CAP]], axis=0)
        b = hop(first if b is None else add(unit, b))
        a = hop(add(jnp.concatenate([mine[CAP:], theirs[CAP:]], axis=0), a))
    handover = swap(jnp.concatenate([b[CAP:], add(b[:CAP], own[CAP:])], axis=0))
    return combine(a, handover, own[:CAP], mixer)


def solution(mesh):
    placed = (
        P(("groups", "ept", "exp"), None),
        P(("groups", "ept", "exp"), None),
        P(("groups", "ept", "exp"), None),
        P("exp", None, "ept"),
        P("exp", None, "ept"),
        P("exp", "ept", None),
    )
    return jax.shard_map(
        body,
        mesh=mesh,
        in_specs=placed,
        out_specs=P(("groups", "ept", "exp"), None),
        check_vma=False,
    )
```

```python
import jax
import jax.numpy as jnp
from jax import lax
from jax.experimental import pallas as pl
from jax.experimental.pallas import tpu as pltpu
from jax.sharding import PartitionSpec as P

CAP = 16
BLOCK = 2 * CAP
LANES = 128
ROWS = 256
VMEM_LIMIT = 8 * 1024 * 1024


def ring_hops(count, cores):
    cycle = [0, 2, 4, 6, 7, 5, 3, 1] if count == 8 else list(range(count))
    hops, across, aside = [], [], []
    for here, there in zip(cycle, cycle[1:] + cycle[:1]):
        for core, (begin, end) in enumerate(((here, there), (there, here))):
            hops.append((begin * cores + core, end * cores + core))
            across.append((begin * cores + core, end * cores + 1 - core))
            aside.append((begin * cores + 1 - core, end * cores + core))
    return hops, across, aside


def swap(value):
    return lax.ppermute(value, "exp", [(0, 1), (1, 0)])


def tile_of(size, most):
    return max(t for t in range(LANES, most + 1, LANES) if size % t == 0)


def in_hbm(value):
    return pltpu.with_memory_space_constraint(value, pltpu.HBM)


def dispatch_kernel(me_ref, ids_ref, weights_ref, tokens_ref, rows_ref, turned_ref, mixer_ref, picker):
    @pl.when(pl.program_id(0) == 0)
    def _():
        token_count = ids_ref.shape[1]
        line = lax.broadcasted_iota(jnp.int32, (BLOCK, token_count), 0)
        expert = (line // CAP + me_ref[0]) % 2
        first = ids_ref[0:1, :] == expert
        second = ids_ref[1:2, :] == expert
        named = first.astype(jnp.float32) + second.astype(jnp.float32)
        row = lax.broadcasted_iota(jnp.int32, (token_count, token_count), 0)
        column = lax.broadcasted_iota(jnp.int32, (token_count, token_count), 1)
        earlier = (row < column).astype(jnp.bfloat16)
        before = jnp.dot(named.astype(jnp.bfloat16), earlier, preferred_element_type=jnp.float32)
        slot = (line % CAP).astype(jnp.float32)
        hit_first = jnp.where(first & (before == slot), 1.0, 0.0)
        after = before + first.astype(jnp.float32)
        hit_second = jnp.where(second & (after == slot), 1.0, 0.0)
        picker[...] = (hit_first + hit_second).astype(jnp.bfloat16)
        mixer = hit_first * weights_ref[0:1, :] + hit_second * weights_ref[1:2, :]
        high = mixer.astype(jnp.bfloat16).astype(jnp.float32)
        empty = jnp.zeros((LANES - 2 * BLOCK, token_count), jnp.float32)
        stacked = jnp.concatenate([high, mixer - high, empty], axis=0)
        mixer_ref[...] = stacked.T.astype(jnp.bfloat16)

    rows = jnp.dot(picker[...], tokens_ref[...], preferred_element_type=jnp.float32)
    rows_ref[...] = rows.astype(jnp.bfloat16)
    turned_ref[:CAP, :] = rows[CAP:].astype(jnp.bfloat16)
    turned_ref[CAP:, :] = rows[:CAP].astype(jnp.bfloat16)


def dispatch(me, expert_ids, route_weights, tokens):
    token_count, width = tokens.shape
    tile = tile_of(width, 3072)
    whole = lambda j, me: (0, 0)
    column = lambda j, me: (0, j)
    return pl.pallas_call(
        dispatch_kernel,
        grid_spec=pltpu.PrefetchScalarGridSpec(
            num_scalar_prefetch=1,
            grid=(width // tile,),
            in_specs=[
                pl.BlockSpec((2, token_count), whole),
                pl.BlockSpec((2, token_count), whole),
                pl.BlockSpec((token_count, tile), column),
            ],
            out_specs=[
                pl.BlockSpec((BLOCK, tile), column),
                pl.BlockSpec((BLOCK, tile), column),
                pl.BlockSpec((token_count, LANES), whole),
            ],
            scratch_shapes=[pltpu.VMEM((BLOCK, token_count), jnp.bfloat16)],
        ),
        out_shape=[
            jax.ShapeDtypeStruct((BLOCK, width), jnp.bfloat16),
            jax.ShapeDtypeStruct((BLOCK, width), jnp.bfloat16),
            jax.ShapeDtypeStruct((token_count, LANES), jnp.bfloat16),
        ],
        compiler_params=pltpu.CompilerParams(vmem_limit_bytes=VMEM_LIMIT),
        name="dispatch",
    )(me, in_hbm(expert_ids.T), in_hbm(route_weights.T), in_hbm(tokens))


def call(kernel, name, operands, outs, scratch=(), flops=0, bytes_accessed=0):
    return pl.pallas_call(
        kernel,
        in_specs=[pl.BlockSpec(memory_space=m) for _, m in operands],
        out_specs=[pl.BlockSpec(memory_space=pltpu.VMEM)] * len(outs),
        out_shape=outs,
        scratch_shapes=scratch,
        cost_estimate=pl.CostEstimate(
            flops=flops, bytes_accessed=bytes_accessed, transcendentals=0
        ),
        compiler_params=pltpu.CompilerParams(vmem_limit_bytes=VMEM_LIMIT),
        name=name,
    )(*[v for v, _ in operands])


def local(*values):
    return [(v, pltpu.VMEM) for v in values]


def held(*values):
    return [(pltpu.with_memory_space_constraint(v, pltpu.VMEM), pltpu.VMEM) for v in values]


def remote(*values):
    return [(in_hbm(v), pltpu.HBM) for v in values]


def array(*shape, dtype=jnp.bfloat16):
    return jax.ShapeDtypeStruct(shape, dtype)


def activate(gate, up):
    return (gate / (1.0 + jnp.exp(-gate)) * up).astype(jnp.bfloat16)


def hold_and_multiply(rows, weights, begin, depth, before):
    width = weights.shape[1]
    total = sum(c for _, _, c in rows)
    step = tile_of(depth, 1536)
    pieces = depth // step
    before = [] if before is None else [before]

    def kernel(*refs):
        row_refs, (source_ref, *refs) = refs[: len(rows)], refs[len(rows) :]
        held_ref, sum_ref, done = refs[len(before) :]
        copies = [
            pltpu.make_async_copy(
                source_ref.at[pl.ds(begin + i * step, step)],
                held_ref.at[pl.ds(i * step, step)],
                done.at[i],
            )
            for i in range(pieces)
        ]
        for copy in copies:
            copy.start()
        for i, copy in enumerate(copies):
            there = slice(begin + i * step, begin + (i + 1) * step)
            block = jnp.concatenate(
                [r[f : f + c, there] for r, (_, f, c) in zip(row_refs, rows)], axis=0
            )
            copy.wait()
            value = jnp.dot(
                block, held_ref[i * step : (i + 1) * step, :], preferred_element_type=jnp.float32
            )
            if i:
                value += sum_ref[...]
            elif before:
                value += refs[0][...]
            sum_ref[...] = value

    return call(
        kernel,
        "hold_and_multiply",
        local(*[r for r, _, _ in rows]) + remote(weights) + local(*before),
        [pltpu.VMEM((depth, width), weights.dtype), array(total, width, dtype=jnp.float32)],
        [pltpu.SemaphoreType.DMA((pieces,))],
        flops=2 * total * depth * width,
        bytes_accessed=2 * depth * width,
    )


def hidden_of(rows, gates, ups, gate_done=None, up_done=None):
    total = sum(c for _, _, c in rows)
    width = gates[0].shape[1]
    tile = tile_of(width, 256)
    before = [] if gate_done is None else [gate_done, up_done]

    def kernel(*refs):
        row_refs, refs = refs[: len(rows)], refs[len(rows) :]
        gate_refs, refs = refs[: len(gates)], refs[len(gates) :]
        up_refs, (*before_refs, out_ref) = refs[: len(ups)], refs[len(ups) :]
        block = jnp.concatenate([r[f : f + c, :] for r, (_, f, c) in zip(row_refs, rows)], axis=0)

        @pl.loop(0, width // tile)
        def _(j):
            here = pl.ds(pl.multiple_of(j * tile, tile), tile)
            values = []
            for i, pieces in enumerate((gate_refs, up_refs)):
                known = before_refs[i].shape[0] if before_refs else 0
                value, first = 0.0, 0
                for ref in pieces:
                    last = first + ref.shape[0]
                    value += jnp.dot(
                        block[known:, first:last], ref[:, here], preferred_element_type=jnp.float32
                    )
                    first = last
                if known:
                    value = jnp.concatenate([before_refs[i][:, here], value], axis=0)
                values.append(value)
            out_ref[:, here] = activate(*values)

    depth = sum(g.shape[0] for g in gates)
    return call(
        kernel,
        "hidden",
        local(*[r for r, _, _ in rows]) + held(*gates, *ups) + local(*before),
        [array(total, width)],
        flops=4 * total * depth * width,
        bytes_accessed=4 * depth * width,
    )[0]


def add(value, *others):
    total = value.astype(jnp.float32)
    for other in others:
        total += other.astype(jnp.float32)
    return total.astype(jnp.bfloat16)


def combine(arrived, handed, product, mixer):
    width = arrived.shape[1]
    token_count = mixer.shape[0]
    tile = tile_of(width, 3072)
    column = lambda j: (0, j)

    def kernel(arrived_ref, handed_ref, product_ref, mixer_ref, out_ref):
        rows = arrived_ref[...].astype(jnp.float32) + handed_ref[...].astype(jnp.float32)
        mine = (rows[:CAP] + product_ref[...].astype(jnp.float32)).astype(jnp.bfloat16)
        theirs = rows[CAP:].astype(jnp.bfloat16)
        rows = jnp.concatenate([mine, theirs, mine, theirs], axis=0)
        out_ref[...] = jnp.dot(
            mixer_ref[:, : 2 * BLOCK], rows, preferred_element_type=jnp.float32
        ).astype(jnp.bfloat16)

    return pl.pallas_call(
        kernel,
        grid=(width // tile,),
        in_specs=[
            pl.BlockSpec((BLOCK, tile), column),
            pl.BlockSpec((BLOCK, tile), column),
            pl.BlockSpec((CAP, tile), column),
            pl.BlockSpec(mixer.shape, lambda j: (0, 0)),
        ],
        out_specs=pl.BlockSpec((token_count, tile), column),
        out_shape=array(token_count, width),
        compiler_params=pltpu.CompilerParams(vmem_limit_bytes=VMEM_LIMIT),
        name="combine",
    )(arrived, handed, product, mixer)


def after(value, other):
    return lax.optimization_barrier((value, other))


def body(tokens, expert_ids, route_weights, w_gate, w_up, w_down):
    ept_count = lax.axis_size("ept")
    hops, across, aside = ring_hops(ept_count, lax.axis_size("exp"))
    reach = ept_count // 2
    w_gate, w_up, w_down = w_gate[0], w_up[0], w_down[0]
    me = lax.axis_index("exp").astype(jnp.int32).reshape(1)

    def hop(value, pairs=hops):
        return lax.ppermute(value, ("ept", "exp"), pairs)

    own, turned, mixer = dispatch(me, expert_ids, route_weights, tokens)
    units = [own, swap(turned)]
    arriving = [hop(units[0]), hop(units[1])]
    plan = [(0, 0, 4, 2, 3, 3), (0, 4, 8, 3, 3, 5), (1, 0, 8, 5, 6, 8)] if ept_count == 8 else []
    weights, held_weights, sums, todo = [w_up, w_gate], [[], []], [None, None], []
    given = [None]
    while len(units) < 2 * reach + 1:
        unit = arriving[len(units) - 2]
        for i, before in list(todo):
            if before == len(units):
                unit, sums[i] = after(unit, sums[i])
                todo.remove((i, before))
        units.append(unit)
        if len(arriving) < 2 * reach - 1:
            arriving.append(hop(unit))
        for i, first, last, newest, count, before in plan:
            if newest == len(units) - 1:
                units[-1], source = after(units[-1], weights[i])
                eighth = source.shape[0] // 8
                rows = [(u, 0, CAP) for u in units[:count]]
                if given[-1] is not None and i == 1:
                    source, given[-1] = after(source, given[-1])
                piece, sums[i] = hold_and_multiply(
                    rows, source, first * eighth, (last - first) * eighth, sums[i]
                )
                held_weights[i].append(piece)
                todo.append((i, before))
        if len(units) == 2 * reach - 2:
            given = [swap(jnp.concatenate([u[CAP:] for u in units[2:]], axis=0))]
    far = swap(jnp.concatenate([u[CAP:] for u in units[-3:]], axis=0))
    ups, gates = (h if h else [w] for h, w in zip(held_weights, weights))
    up_done, gate_done = sums

    rows = [(u, 0, CAP) for u in units[:-1]]
    rows += [(given[0], BLOCK * k, BLOCK) for k in range(reach - 2)] + [(far, 0, BLOCK)]
    rows += [(units[-1], 0, CAP), (far, BLOCK, CAP)]
    groups = [[]]
    for row in rows:
        if sum(c for _, _, c in groups[-1]) + row[2] > ROWS:
            groups.append([])
        groups[-1].append(row)
    hidden = [hidden_of(groups[0], gates, ups, gate_done, up_done)]
    hidden += [hidden_of(group, gates, ups) for group in groups[1:]]
    hidden = jnp.concatenate(hidden, axis=0) if len(hidden) > 1 else hidden[0]
    mine = [hidden[BLOCK * k : BLOCK * (k + 1)] for k in range(reach)]
    others = [hidden[BLOCK * k : BLOCK * (k + 1)] for k in range(reach, 2 * reach)]

    def product_of(*parts):
        product = jnp.dot(
            jnp.concatenate(parts, axis=0), w_down, preferred_element_type=jnp.float32
        )
        return lax.optimization_barrier(product.astype(jnp.bfloat16))

    product = product_of(mine[reach - 1], *others[-2:])
    handed, kept = [swap(product[:BLOCK])], [product[BLOCK : 2 * BLOCK]]
    a = [hop(product[2 * BLOCK : 2 * BLOCK + CAP]), hop(product[2 * BLOCK + CAP :], aside)]
    first = jnp.concatenate([kept[0][:CAP], handed[0][:CAP]], axis=0)
    first, parts = after(first, (*mine[:-1], *others[:-2]))
    product = product_of(*parts)
    a, product = after(a, product)
    own = product[:BLOCK]
    if reach > 2:
        more = swap(product[BLOCK : BLOCK * (reach - 1)])
        handed += [more[BLOCK * k : BLOCK * (k + 1)] for k in reversed(range(reach - 2))]
        more = product[BLOCK * (reach - 1) :]
        kept += [more[BLOCK * k : BLOCK * (k + 1)] for k in reversed(range(reach - 2))]
    b = None
    for mine, theirs in zip(kept, handed):
        unit = jnp.concatenate([mine[:CAP], theirs[:CAP]], axis=0)
        b = hop(first if b is None else add(unit, b))
        if isinstance(a, list):
            a = jnp.concatenate(a, axis=0)
        a = hop(add(jnp.concatenate([mine[CAP:], theirs[CAP:]], axis=0), a))
    handover = swap(jnp.concatenate([b[CAP:], add(b[:CAP], own[CAP:])], axis=0))
    return combine(a, handover, own[:CAP], mixer)


def solution(mesh):
    placed = (
        P(("groups", "ept", "exp"), None),
        P(("groups", "ept", "exp"), None),
        P(("groups", "ept", "exp"), None),
        P("exp", None, "ept"),
        P("exp", None, "ept"),
        P("exp", "ept", None),
    )
    return jax.shard_map(
        body,
        mesh=mesh,
        in_specs=placed,
        out_specs=P(("groups", "ept", "exp"), None),
        check_vma=False,
    )
```

```python
import jax
import jax.numpy as jnp
from jax import lax
from jax.experimental import pallas as pl
from jax.experimental.pallas import tpu as pltpu
from jax.sharding import PartitionSpec as P

CAP = 16
BLOCK = 2 * CAP
LANES = 128
ROWS = 256
VMEM_LIMIT = 8 * 1024 * 1024


def ring_hops(count, cores):
    cycle = [0, 2, 4, 6, 7, 5, 3, 1] if count == 8 else list(range(count))
    hops, across, aside = [], [], []
    for here, there in zip(cycle, cycle[1:] + cycle[:1]):
        for core, (begin, end) in enumerate(((here, there), (there, here))):
            hops.append((begin * cores + core, end * cores + core))
            across.append((begin * cores + core, end * cores + 1 - core))
            aside.append((begin * cores + 1 - core, end * cores + core))
    return hops, across, aside


def swap(value):
    return lax.ppermute(value, "exp", [(0, 1), (1, 0)])


def tile_of(size, most):
    return max(t for t in range(LANES, most + 1, LANES) if size % t == 0)


def in_hbm(value):
    return pltpu.with_memory_space_constraint(value, pltpu.HBM)


def dispatch_kernel(me_ref, ids_ref, weights_ref, tokens_ref, rows_ref, turned_ref, mixer_ref, picker):
    @pl.when(pl.program_id(0) == 0)
    def _():
        token_count = ids_ref.shape[1]
        line = lax.broadcasted_iota(jnp.int32, (BLOCK, token_count), 0)
        expert = (line // CAP + me_ref[0]) % 2
        first = ids_ref[0:1, :] == expert
        second = ids_ref[1:2, :] == expert
        named = first.astype(jnp.float32) + second.astype(jnp.float32)
        row = lax.broadcasted_iota(jnp.int32, (token_count, token_count), 0)
        column = lax.broadcasted_iota(jnp.int32, (token_count, token_count), 1)
        earlier = (row < column).astype(jnp.bfloat16)
        before = jnp.dot(named.astype(jnp.bfloat16), earlier, preferred_element_type=jnp.float32)
        slot = (line % CAP).astype(jnp.float32)
        hit_first = jnp.where(first & (before == slot), 1.0, 0.0)
        after = before + first.astype(jnp.float32)
        hit_second = jnp.where(second & (after == slot), 1.0, 0.0)
        picker[...] = (hit_first + hit_second).astype(jnp.bfloat16)
        mixer = hit_first * weights_ref[0:1, :] + hit_second * weights_ref[1:2, :]
        high = mixer.astype(jnp.bfloat16).astype(jnp.float32)
        empty = jnp.zeros((LANES - 2 * BLOCK, token_count), jnp.float32)
        stacked = jnp.concatenate([high, mixer - high, empty], axis=0)
        mixer_ref[...] = stacked.T.astype(jnp.bfloat16)

    rows = jnp.dot(picker[...], tokens_ref[...], preferred_element_type=jnp.float32)
    rows_ref[...] = rows.astype(jnp.bfloat16)
    turned_ref[:CAP, :] = rows[CAP:].astype(jnp.bfloat16)
    turned_ref[CAP:, :] = rows[:CAP].astype(jnp.bfloat16)


def dispatch(me, expert_ids, route_weights, tokens):
    token_count, width = tokens.shape
    tile = tile_of(width, 3072)
    whole = lambda j, me: (0, 0)
    column = lambda j, me: (0, j)
    return pl.pallas_call(
        dispatch_kernel,
        grid_spec=pltpu.PrefetchScalarGridSpec(
            num_scalar_prefetch=1,
            grid=(width // tile,),
            in_specs=[
                pl.BlockSpec((2, token_count), whole),
                pl.BlockSpec((2, token_count), whole),
                pl.BlockSpec((token_count, tile), column),
            ],
            out_specs=[
                pl.BlockSpec((BLOCK, tile), column),
                pl.BlockSpec((BLOCK, tile), column),
                pl.BlockSpec((token_count, LANES), whole),
            ],
            scratch_shapes=[pltpu.VMEM((BLOCK, token_count), jnp.bfloat16)],
        ),
        out_shape=[
            jax.ShapeDtypeStruct((BLOCK, width), jnp.bfloat16),
            jax.ShapeDtypeStruct((BLOCK, width), jnp.bfloat16),
            jax.ShapeDtypeStruct((token_count, LANES), jnp.bfloat16),
        ],
        compiler_params=pltpu.CompilerParams(vmem_limit_bytes=VMEM_LIMIT),
        name="dispatch",
    )(me, in_hbm(expert_ids.T), in_hbm(route_weights.T), in_hbm(tokens))


def call(kernel, name, operands, outs, scratch=(), flops=0, bytes_accessed=0):
    return pl.pallas_call(
        kernel,
        in_specs=[pl.BlockSpec(memory_space=m) for _, m in operands],
        out_specs=[pl.BlockSpec(memory_space=pltpu.VMEM)] * len(outs),
        out_shape=outs,
        scratch_shapes=scratch,
        cost_estimate=pl.CostEstimate(
            flops=flops, bytes_accessed=bytes_accessed, transcendentals=0
        ),
        compiler_params=pltpu.CompilerParams(vmem_limit_bytes=VMEM_LIMIT),
        name=name,
    )(*[v for v, _ in operands])


def local(*values):
    return [(v, pltpu.VMEM) for v in values]


def held(*values):
    return [(pltpu.with_memory_space_constraint(v, pltpu.VMEM), pltpu.VMEM) for v in values]


def remote(*values):
    return [(in_hbm(v), pltpu.HBM) for v in values]


def array(*shape, dtype=jnp.bfloat16):
    return jax.ShapeDtypeStruct(shape, dtype)


def activate(gate, up):
    return (gate / (1.0 + jnp.exp(-gate)) * up).astype(jnp.bfloat16)


def hold_and_multiply(rows, weights, begin, depth, before):
    width = weights.shape[1]
    total = sum(c for _, _, c in rows)
    step = tile_of(depth, 768)
    pieces = depth // step
    before = [] if before is None else [before]

    def kernel(*refs):
        row_refs, (source_ref, *refs) = refs[: len(rows)], refs[len(rows) :]
        held_ref, sum_ref, done = refs[len(before) :]
        copies = [
            pltpu.make_async_copy(
                source_ref.at[pl.ds(begin + i * step, step)],
                held_ref.at[pl.ds(i * step, step)],
                done.at[i],
            )
            for i in range(pieces)
        ]
        for copy in copies:
            copy.start()
        for i, copy in enumerate(copies):
            there = slice(begin + i * step, begin + (i + 1) * step)
            block = jnp.concatenate(
                [r[f : f + c, there] for r, (_, f, c) in zip(row_refs, rows)], axis=0
            )
            copy.wait()
            value = jnp.dot(
                block, held_ref[i * step : (i + 1) * step, :], preferred_element_type=jnp.float32
            )
            if i:
                value += sum_ref[...]
            elif before:
                value += refs[0][...]
            sum_ref[...] = value

    return call(
        kernel,
        "hold_and_multiply",
        local(*[r for r, _, _ in rows]) + remote(weights) + local(*before),
        [pltpu.VMEM((depth, width), weights.dtype), array(total, width, dtype=jnp.float32)],
        [pltpu.SemaphoreType.DMA((pieces,))],
        flops=2 * total * depth * width,
        bytes_accessed=2 * depth * width,
    )


def hidden_of(rows, gates, ups, gate_done=None, up_done=None):
    total = sum(c for _, _, c in rows)
    width = gates[0].shape[1]
    tile = tile_of(width, 1024)
    before = [] if gate_done is None else [gate_done, up_done]

    def kernel(*refs):
        row_refs, refs = refs[: len(rows)], refs[len(rows) :]
        gate_refs, refs = refs[: len(gates)], refs[len(gates) :]
        up_refs, (*before_refs, out_ref) = refs[: len(ups)], refs[len(ups) :]
        block = jnp.concatenate([r[f : f + c, :] for r, (_, f, c) in zip(row_refs, rows)], axis=0)

        @pl.loop(0, width // tile)
        def _(j):
            here = pl.ds(pl.multiple_of(j * tile, tile), tile)
            values = []
            for i, pieces in enumerate((gate_refs, up_refs)):
                known = before_refs[i].shape[0] if before_refs else 0
                value, first = 0.0, 0
                for ref in pieces:
                    last = first + ref.shape[0]
                    value += jnp.dot(
                        block[known:, first:last], ref[:, here], preferred_element_type=jnp.float32
                    )
                    first = last
                if known:
                    value = jnp.concatenate([before_refs[i][:, here], value], axis=0)
                values.append(value)
            out_ref[:, here] = activate(*values)

    depth = sum(g.shape[0] for g in gates)
    return call(
        kernel,
        "hidden",
        local(*[r for r, _, _ in rows]) + held(*gates, *ups) + local(*before),
        [array(total, width)],
        flops=4 * total * depth * width,
        bytes_accessed=4 * depth * width,
    )[0]


def add(value, *others):
    total = value.astype(jnp.float32)
    for other in others:
        total += other.astype(jnp.float32)
    return total.astype(jnp.bfloat16)


def combine(arrived, handed, product, mixer):
    width = arrived.shape[1]
    token_count = mixer.shape[0]
    tile = tile_of(width, 1536)
    steps = width // tile

    def kernel(arrived_ref, handed_ref, product_ref, mixer_ref, out_hbm, mixed_ref, done):
        copies = []
        for i in range(steps):
            here = slice(i * tile, (i + 1) * tile)
            rows = arrived_ref[:, here].astype(jnp.float32) + handed_ref[:, here].astype(
                jnp.float32
            )
            mine = (rows[:CAP] + product_ref[:CAP, here].astype(jnp.float32)).astype(jnp.bfloat16)
            theirs = rows[CAP:].astype(jnp.bfloat16)
            rows = jnp.concatenate([mine, theirs, mine, theirs], axis=0)
            mixed_ref[:, here] = jnp.dot(
                mixer_ref[:, : 2 * BLOCK], rows, preferred_element_type=jnp.float32
            ).astype(jnp.bfloat16)
            copies.append(
                pltpu.make_async_copy(
                    mixed_ref.at[:, pl.ds(i * tile, tile)],
                    out_hbm.at[:, pl.ds(i * tile, tile)],
                    done.at[i],
                )
            )
            copies[i].start()
        for copy in copies:
            copy.wait()

    local_spec = pl.BlockSpec(memory_space=pltpu.VMEM)
    return pl.pallas_call(
        kernel,
        in_specs=[local_spec] * 4,
        out_specs=pl.BlockSpec(memory_space=pltpu.HBM),
        out_shape=array(token_count, width),
        scratch_shapes=[
            pltpu.VMEM((token_count, width), jnp.bfloat16),
            pltpu.SemaphoreType.DMA((steps,)),
        ],
        compiler_params=pltpu.CompilerParams(vmem_limit_bytes=VMEM_LIMIT),
        name="combine",
    )(arrived, handed, product, mixer)


def after(value, other):
    return lax.optimization_barrier((value, other))


def body(tokens, expert_ids, route_weights, w_gate, w_up, w_down):
    ept_count = lax.axis_size("ept")
    hops, across, aside = ring_hops(ept_count, lax.axis_size("exp"))
    reach = ept_count // 2
    w_gate, w_up, w_down = w_gate[0], w_up[0], w_down[0]
    me = lax.axis_index("exp").astype(jnp.int32).reshape(1)

    def hop(value, pairs=hops):
        return lax.ppermute(value, ("ept", "exp"), pairs)

    own, turned, mixer = dispatch(me, expert_ids, route_weights, tokens)
    units = [own, swap(turned)]
    arriving = [hop(units[0]), hop(units[1])]
    plan = [(0, 0, 4, 2, 3, 3), (0, 4, 8, 3, 3, 5), (1, 0, 8, 5, 6, 8)] if ept_count == 8 else []
    weights, held_weights, sums, todo = [w_up, w_gate], [[], []], [None, None], []
    given = [None]
    while len(units) < 2 * reach + 1:
        unit = arriving[len(units) - 2]
        for i, before in list(todo):
            if before == len(units):
                unit, sums[i] = after(unit, sums[i])
                todo.remove((i, before))
        units.append(unit)
        if len(arriving) < 2 * reach - 1:
            arriving.append(hop(unit))
        for i, first, last, newest, count, before in plan:
            if newest == len(units) - 1:
                units[-1], source = after(units[-1], weights[i])
                eighth = source.shape[0] // 8
                rows = [(u, 0, CAP) for u in units[:count]]
                if given[-1] is not None and i == 1:
                    source, given[-1] = after(source, given[-1])
                piece, sums[i] = hold_and_multiply(
                    rows, source, first * eighth, (last - first) * eighth, sums[i]
                )
                held_weights[i].append(piece)
                todo.append((i, before))
        if len(units) == 2 * reach - 2:
            given = [swap(jnp.concatenate([u[CAP:] for u in units[2:]], axis=0))]
    far = swap(jnp.concatenate([u[CAP:] for u in units[-3:]], axis=0))
    ups, gates = (h if h else [w] for h, w in zip(held_weights, weights))
    up_done, gate_done = sums

    rows = [(u, 0, CAP) for u in units[:-1]]
    rows += [(given[0], BLOCK * k, BLOCK) for k in range(reach - 2)] + [(far, 0, BLOCK)]
    rows += [(units[-1], 0, CAP), (far, BLOCK, CAP)]
    groups = [[]]
    for row in rows:
        if sum(c for _, _, c in groups[-1]) + row[2] > ROWS:
            groups.append([])
        groups[-1].append(row)
    hidden = [hidden_of(groups[0], gates, ups, gate_done, up_done)]
    hidden += [hidden_of(group, gates, ups) for group in groups[1:]]
    hidden = jnp.concatenate(hidden, axis=0) if len(hidden) > 1 else hidden[0]
    mine = [hidden[BLOCK * k : BLOCK * (k + 1)] for k in range(reach)]
    others = [hidden[BLOCK * k : BLOCK * (k + 1)] for k in range(reach, 2 * reach)]

    def product_of(*parts):
        product = jnp.dot(
            jnp.concatenate(parts, axis=0), w_down, preferred_element_type=jnp.float32
        )
        return lax.optimization_barrier(product.astype(jnp.bfloat16))

    product = product_of(mine[reach - 1], *others[-2:])
    handed, kept = [swap(product[:BLOCK])], [product[BLOCK : 2 * BLOCK]]
    a = [hop(product[2 * BLOCK : 2 * BLOCK + CAP]), hop(product[2 * BLOCK + CAP :], aside)]
    first = jnp.concatenate([kept[0][:CAP], handed[0][:CAP]], axis=0)
    first, parts = after(first, (*mine[:-1], *others[:-2]))
    product = product_of(*parts)
    a, product = after(a, product)
    own = product[:BLOCK]
    if reach > 2:
        more = swap(product[BLOCK : BLOCK * (reach - 1)])
        handed += [more[BLOCK * k : BLOCK * (k + 1)] for k in reversed(range(reach - 2))]
        more = product[BLOCK * (reach - 1) :]
        kept += [more[BLOCK * k : BLOCK * (k + 1)] for k in reversed(range(reach - 2))]
    b = None
    for mine, theirs in zip(kept, handed):
        unit = jnp.concatenate([mine[:CAP], theirs[:CAP]], axis=0)
        b = hop(first if b is None else add(unit, b))
        if isinstance(a, list):
            a = jnp.concatenate(a, axis=0)
        a = hop(add(jnp.concatenate([mine[CAP:], theirs[CAP:]], axis=0), a))
    handover = swap(jnp.concatenate([b[CAP:], add(b[:CAP], own[CAP:])], axis=0))
    return combine(a, handover, own[:CAP], mixer)


def solution(mesh):
    placed = (
        P(("groups", "ept", "exp"), None),
        P(("groups", "ept", "exp"), None),
        P(("groups", "ept", "exp"), None),
        P("exp", None, "ept"),
        P("exp", None, "ept"),
        P("exp", "ept", None),
    )
    return jax.shard_map(
        body,
        mesh=mesh,
        in_specs=placed,
        out_specs=P(("groups", "ept", "exp"), None),
        check_vma=False,
    )
```

```python
import jax
import jax.numpy as jnp
from jax import lax
from jax.experimental import pallas as pl
from jax.experimental.pallas import tpu as pltpu
from jax.sharding import PartitionSpec as P

CAP = 16
BLOCK = 2 * CAP
LANES = 128
ROWS = 256
VMEM_LIMIT = 8 * 1024 * 1024


def ring_hops(count, cores):
    cycle = [0, 2, 4, 6, 7, 5, 3, 1] if count == 8 else list(range(count))
    hops, across, aside = [], [], []
    for here, there in zip(cycle, cycle[1:] + cycle[:1]):
        for core, (begin, end) in enumerate(((here, there), (there, here))):
            hops.append((begin * cores + core, end * cores + core))
            across.append((begin * cores + core, end * cores + 1 - core))
            aside.append((begin * cores + 1 - core, end * cores + core))
    return hops, across, aside


def swap(value):
    return lax.ppermute(value, "exp", [(0, 1), (1, 0)])


def tile_of(size, most):
    return max(t for t in range(LANES, most + 1, LANES) if size % t == 0)


def in_hbm(value):
    return pltpu.with_memory_space_constraint(value, pltpu.HBM)


def dispatch_kernel(me_ref, ids_ref, weights_ref, tokens_ref, rows_ref, turned_ref, mixer_ref, picker):
    @pl.when(pl.program_id(0) == 0)
    def _():
        token_count = ids_ref.shape[1]
        line = lax.broadcasted_iota(jnp.int32, (BLOCK, token_count), 0)
        expert = (line // CAP + me_ref[0]) % 2
        first = ids_ref[0:1, :] == expert
        second = ids_ref[1:2, :] == expert
        named = first.astype(jnp.float32) + second.astype(jnp.float32)
        row = lax.broadcasted_iota(jnp.int32, (token_count, token_count), 0)
        column = lax.broadcasted_iota(jnp.int32, (token_count, token_count), 1)
        earlier = (row < column).astype(jnp.bfloat16)
        before = jnp.dot(named.astype(jnp.bfloat16), earlier, preferred_element_type=jnp.float32)
        slot = (line % CAP).astype(jnp.float32)
        hit_first = jnp.where(first & (before == slot), 1.0, 0.0)
        after = before + first.astype(jnp.float32)
        hit_second = jnp.where(second & (after == slot), 1.0, 0.0)
        picker[...] = (hit_first + hit_second).astype(jnp.bfloat16)
        mixer = hit_first * weights_ref[0:1, :] + hit_second * weights_ref[1:2, :]
        high = mixer.astype(jnp.bfloat16).astype(jnp.float32)
        empty = jnp.zeros((LANES - 2 * BLOCK, token_count), jnp.float32)
        stacked = jnp.concatenate([high, mixer - high, empty], axis=0)
        mixer_ref[...] = stacked.T.astype(jnp.bfloat16)

    rows = jnp.dot(picker[...], tokens_ref[...], preferred_element_type=jnp.float32)
    rows_ref[...] = rows.astype(jnp.bfloat16)
    turned_ref[:CAP, :] = rows[CAP:].astype(jnp.bfloat16)
    turned_ref[CAP:, :] = rows[:CAP].astype(jnp.bfloat16)


def dispatch(me, expert_ids, route_weights, tokens):
    token_count, width = tokens.shape
    tile = tile_of(width, 3072)
    whole = lambda j, me: (0, 0)
    column = lambda j, me: (0, j)
    return pl.pallas_call(
        dispatch_kernel,
        grid_spec=pltpu.PrefetchScalarGridSpec(
            num_scalar_prefetch=1,
            grid=(width // tile,),
            in_specs=[
                pl.BlockSpec((2, token_count), whole),
                pl.BlockSpec((2, token_count), whole),
                pl.BlockSpec((token_count, tile), column),
            ],
            out_specs=[
                pl.BlockSpec((BLOCK, tile), column),
                pl.BlockSpec((BLOCK, tile), column),
                pl.BlockSpec((token_count, LANES), whole),
            ],
            scratch_shapes=[pltpu.VMEM((BLOCK, token_count), jnp.bfloat16)],
        ),
        out_shape=[
            jax.ShapeDtypeStruct((BLOCK, width), jnp.bfloat16),
            jax.ShapeDtypeStruct((BLOCK, width), jnp.bfloat16),
            jax.ShapeDtypeStruct((token_count, LANES), jnp.bfloat16),
        ],
        compiler_params=pltpu.CompilerParams(vmem_limit_bytes=VMEM_LIMIT),
        name="dispatch",
    )(me, in_hbm(expert_ids.T), in_hbm(route_weights.T), in_hbm(tokens))


def call(kernel, name, operands, outs, scratch=(), flops=0, bytes_accessed=0):
    return pl.pallas_call(
        kernel,
        in_specs=[pl.BlockSpec(memory_space=m) for _, m in operands],
        out_specs=[pl.BlockSpec(memory_space=pltpu.VMEM)] * len(outs),
        out_shape=outs,
        scratch_shapes=scratch,
        cost_estimate=pl.CostEstimate(
            flops=flops, bytes_accessed=bytes_accessed, transcendentals=0
        ),
        compiler_params=pltpu.CompilerParams(vmem_limit_bytes=VMEM_LIMIT),
        name=name,
    )(*[v for v, _ in operands])


def local(*values):
    return [(v, pltpu.VMEM) for v in values]


def held(*values):
    return [(pltpu.with_memory_space_constraint(v, pltpu.VMEM), pltpu.VMEM) for v in values]


def remote(*values):
    return [(in_hbm(v), pltpu.HBM) for v in values]


def array(*shape, dtype=jnp.bfloat16):
    return jax.ShapeDtypeStruct(shape, dtype)


def activate(gate, up):
    return (gate / (1.0 + jnp.exp(-gate)) * up).astype(jnp.bfloat16)


def hold_and_multiply(rows, weights, begin, depth, before):
    width = weights.shape[1]
    total = sum(c for _, _, c in rows)
    step = tile_of(depth, 384)
    pieces = depth // step
    before = [] if before is None else [before]

    def kernel(*refs):
        row_refs, (source_ref, *refs) = refs[: len(rows)], refs[len(rows) :]
        held_ref, sum_ref, done = refs[len(before) :]
        copies = [
            pltpu.make_async_copy(
                source_ref.at[pl.ds(begin + i * step, step)],
                held_ref.at[pl.ds(i * step, step)],
                done.at[i],
            )
            for i in range(pieces)
        ]
        for copy in copies:
            copy.start()
        for i, copy in enumerate(copies):
            there = slice(begin + i * step, begin + (i + 1) * step)
            block = jnp.concatenate(
                [r[f : f + c, there] for r, (_, f, c) in zip(row_refs, rows)], axis=0
            )
            copy.wait()
            value = jnp.dot(
                block, held_ref[i * step : (i + 1) * step, :], preferred_element_type=jnp.float32
            )
            if i:
                value += sum_ref[...]
            elif before:
                value += refs[0][...]
            sum_ref[...] = value

    return call(
        kernel,
        "hold_and_multiply",
        local(*[r for r, _, _ in rows]) + remote(weights) + local(*before),
        [pltpu.VMEM((depth, width), weights.dtype), array(total, width, dtype=jnp.float32)],
        [pltpu.SemaphoreType.DMA((pieces,))],
        flops=2 * total * depth * width,
        bytes_accessed=2 * depth * width,
    )


def hidden_of(rows, gates, ups, gate_done=None, up_done=None):
    total = sum(c for _, _, c in rows)
    width = gates[0].shape[1]
    tile = tile_of(width, 1024)
    before = [] if gate_done is None else [gate_done, up_done]

    def kernel(*refs):
        row_refs, refs = refs[: len(rows)], refs[len(rows) :]
        gate_refs, refs = refs[: len(gates)], refs[len(gates) :]
        up_refs, (*before_refs, out_ref) = refs[: len(ups)], refs[len(ups) :]
        block = jnp.concatenate([r[f : f + c, :] for r, (_, f, c) in zip(row_refs, rows)], axis=0)

        @pl.loop(0, width // tile)
        def _(j):
            here = pl.ds(pl.multiple_of(j * tile, tile), tile)
            values = []
            for i, pieces in enumerate((gate_refs, up_refs)):
                known = before_refs[i].shape[0] if before_refs else 0
                value, first = 0.0, 0
                for ref in pieces:
                    last = first + ref.shape[0]
                    value += jnp.dot(
                        block[known:, first:last], ref[:, here], preferred_element_type=jnp.float32
                    )
                    first = last
                if known:
                    value = jnp.concatenate([before_refs[i][:, here], value], axis=0)
                values.append(value)
            out_ref[:, here] = activate(*values)

    depth = sum(g.shape[0] for g in gates)
    return call(
        kernel,
        "hidden",
        local(*[r for r, _, _ in rows]) + held(*gates, *ups) + local(*before),
        [array(total, width)],
        flops=4 * total * depth * width,
        bytes_accessed=4 * depth * width,
    )[0]


def add(value, *others):
    total = value.astype(jnp.float32)
    for other in others:
        total += other.astype(jnp.float32)
    return total.astype(jnp.bfloat16)


def combine(arrived, handed, product, mixer):
    width = arrived.shape[1]
    token_count = mixer.shape[0]
    tile = tile_of(width, 1536)
    steps = width // tile

    def kernel(arrived_ref, handed_ref, product_ref, mixer_ref, out_hbm, mixed_ref, done):
        copies = []
        for i in range(steps):
            here = slice(i * tile, (i + 1) * tile)
            rows = arrived_ref[:, here].astype(jnp.float32) + handed_ref[:, here].astype(
                jnp.float32
            )
            mine = (rows[:CAP] + product_ref[:CAP, here].astype(jnp.float32)).astype(jnp.bfloat16)
            theirs = rows[CAP:].astype(jnp.bfloat16)
            rows = jnp.concatenate([mine, theirs, mine, theirs], axis=0)
            mixed_ref[:, here] = jnp.dot(
                mixer_ref[:, : 2 * BLOCK], rows, preferred_element_type=jnp.float32
            ).astype(jnp.bfloat16)
            copies.append(
                pltpu.make_async_copy(
                    mixed_ref.at[:, pl.ds(i * tile, tile)],
                    out_hbm.at[:, pl.ds(i * tile, tile)],
                    done.at[i],
                )
            )
            copies[i].start()
        for copy in copies:
            copy.wait()

    local_spec = pl.BlockSpec(memory_space=pltpu.VMEM)
    return pl.pallas_call(
        kernel,
        in_specs=[local_spec] * 4,
        out_specs=pl.BlockSpec(memory_space=pltpu.HBM),
        out_shape=array(token_count, width),
        scratch_shapes=[
            pltpu.VMEM((token_count, width), jnp.bfloat16),
            pltpu.SemaphoreType.DMA((steps,)),
        ],
        compiler_params=pltpu.CompilerParams(vmem_limit_bytes=VMEM_LIMIT),
        name="combine",
    )(arrived, handed, product, mixer)


def after(value, other):
    return lax.optimization_barrier((value, other))


def body(tokens, expert_ids, route_weights, w_gate, w_up, w_down):
    ept_count = lax.axis_size("ept")
    hops, across, aside = ring_hops(ept_count, lax.axis_size("exp"))
    reach = ept_count // 2
    w_gate, w_up, w_down = w_gate[0], w_up[0], w_down[0]
    me = lax.axis_index("exp").astype(jnp.int32).reshape(1)

    def hop(value, pairs=hops):
        return lax.ppermute(value, ("ept", "exp"), pairs)

    own, turned, mixer = dispatch(me, expert_ids, route_weights, tokens)
    units = [own, swap(turned)]
    arriving = [hop(units[0]), hop(units[1])]
    plan = [(0, 0, 3, 2, 3, 3), (0, 3, 6, 3, 3, 4), (0, 6, 8, 4, 3, 5), (1, 0, 3, 5, 6, 6), (1, 3, 8, 6, 6, 8)] if ept_count == 8 else []
    weights, held_weights, sums, todo = [w_up, w_gate], [[], []], [None, None], []
    given = [None]
    while len(units) < 2 * reach + 1:
        unit = arriving[len(units) - 2]
        for i, before in list(todo):
            if before == len(units):
                unit, sums[i] = after(unit, sums[i])
                todo.remove((i, before))
        units.append(unit)
        if len(arriving) < 2 * reach - 1:
            arriving.append(hop(unit))
        for i, first, last, newest, count, before in plan:
            if newest == len(units) - 1:
                units[-1], source = after(units[-1], weights[i])
                eighth = source.shape[0] // 8
                rows = [(u, 0, CAP) for u in units[:count]]
                if given[-1] is not None and i == 1:
                    source, given[-1] = after(source, given[-1])
                piece, sums[i] = hold_and_multiply(
                    rows, source, first * eighth, (last - first) * eighth, sums[i]
                )
                held_weights[i].append(piece)
                todo.append((i, before))
        if len(units) == 2 * reach - 2:
            given = [swap(jnp.concatenate([u[CAP:] for u in units[2:]], axis=0))]
    given.append(swap(jnp.concatenate([u[CAP:] for u in units[-3:-1]], axis=0)))
    far = swap(units[-1][CAP:])
    ups, gates = (h if h else [w] for h, w in zip(held_weights, weights))
    up_done, gate_done = sums

    rows = [(u, 0, CAP) for u in units[:-1]]
    rows += [(given[0], BLOCK * k, BLOCK) for k in range(reach - 2)] + [(given[1], 0, BLOCK)]
    rows += [(units[-1], 0, CAP), (far, 0, CAP)]
    groups = [[]]
    for row in rows:
        if sum(c for _, _, c in groups[-1]) + row[2] > ROWS:
            groups.append([])
        groups[-1].append(row)
    hidden = [hidden_of(groups[0], gates, ups, gate_done, up_done)]
    hidden += [hidden_of(group, gates, ups) for group in groups[1:]]
    hidden = jnp.concatenate(hidden, axis=0) if len(hidden) > 1 else hidden[0]
    mine = [hidden[BLOCK * k : BLOCK * (k + 1)] for k in range(reach)]
    others = [hidden[BLOCK * k : BLOCK * (k + 1)] for k in range(reach, 2 * reach)]

    def product_of(*parts):
        product = jnp.dot(
            jnp.concatenate(parts, axis=0), w_down, preferred_element_type=jnp.float32
        )
        return lax.optimization_barrier(product.astype(jnp.bfloat16))

    product = product_of(mine[reach - 1], *others[-2:])
    handed, kept = [swap(product[:BLOCK])], [product[BLOCK : 2 * BLOCK]]
    a = [hop(product[2 * BLOCK : 2 * BLOCK + CAP]), hop(product[2 * BLOCK + CAP :], aside)]
    first = jnp.concatenate([kept[0][:CAP], handed[0][:CAP]], axis=0)
    first, parts = after(first, (*mine[:-1], *others[:-2]))
    product = product_of(*parts)
    a, product = after(a, product)
    own = product[:BLOCK]
    if reach > 2:
        more = swap(product[BLOCK : BLOCK * (reach - 1)])
        handed += [more[BLOCK * k : BLOCK * (k + 1)] for k in reversed(range(reach - 2))]
        more = product[BLOCK * (reach - 1) :]
        kept += [more[BLOCK * k : BLOCK * (k + 1)] for k in reversed(range(reach - 2))]
    b = None
    for mine, theirs in zip(kept, handed):
        unit = jnp.concatenate([mine[:CAP], theirs[:CAP]], axis=0)
        b = hop(first if b is None else add(unit, b))
        if isinstance(a, list):
            a = jnp.concatenate(a, axis=0)
        a = hop(add(jnp.concatenate([mine[CAP:], theirs[CAP:]], axis=0), a))
    handover = swap(jnp.concatenate([b[CAP:], add(b[:CAP], own[CAP:])], axis=0))
    return combine(a, handover, own[:CAP], mixer)


def solution(mesh):
    placed = (
        P(("groups", "ept", "exp"), None),
        P(("groups", "ept", "exp"), None),
        P(("groups", "ept", "exp"), None),
        P("exp", None, "ept"),
        P("exp", None, "ept"),
        P("exp", "ept", None),
    )
    return jax.shard_map(
        body,
        mesh=mesh,
        in_specs=placed,
        out_specs=P(("groups", "ept", "exp"), None),
        check_vma=False,
    )
```

```python
import jax
import jax.numpy as jnp
from jax import lax
from jax.experimental import pallas as pl
from jax.experimental.pallas import tpu as pltpu
from jax.sharding import PartitionSpec as P

CAP = 16
BLOCK = 2 * CAP
LANES = 128
ROWS = 256
VMEM_LIMIT = 8 * 1024 * 1024


def ring_hops(count, cores):
    cycle = [0, 2, 4, 6, 7, 5, 3, 1] if count == 8 else list(range(count))
    hops, across, aside = [], [], []
    for here, there in zip(cycle, cycle[1:] + cycle[:1]):
        for core, (begin, end) in enumerate(((here, there), (there, here))):
            hops.append((begin * cores + core, end * cores + core))
            across.append((begin * cores + core, end * cores + 1 - core))
            aside.append((begin * cores + 1 - core, end * cores + core))
    return hops, across, aside


def swap(value):
    return lax.ppermute(value, "exp", [(0, 1), (1, 0)])


def tile_of(size, most):
    return max(t for t in range(LANES, most + 1, LANES) if size % t == 0)


def in_hbm(value):
    return pltpu.with_memory_space_constraint(value, pltpu.HBM)


def dispatch(me, expert_ids, route_weights, tokens):
    token_count, width = tokens.shape
    tile = tile_of(width, 3072)
    steps = width // tile

    def kernel(me_ref, ids_hbm, weights_hbm, tokens_hbm, rows_ref, turned_ref, mixer_ref, *scratch):
        ids_ref, weights_ref, held_ref, done = scratch
        copies = [
            pltpu.make_async_copy(ids_hbm, ids_ref, done.at[0]),
            pltpu.make_async_copy(weights_hbm, weights_ref, done.at[1]),
        ]
        for i in range(steps):
            here = pl.ds(i * tile, tile)
            copies.append(
                pltpu.make_async_copy(
                    tokens_hbm.at[:, here], held_ref.at[:, here], done.at[2 + i]
                )
            )
        for copy in copies:
            copy.start()
        line = lax.broadcasted_iota(jnp.int32, (BLOCK, token_count), 0)
        expert = (line // CAP + me_ref[0]) % 2
        slot = (line % CAP).astype(jnp.float32)
        row = lax.broadcasted_iota(jnp.int32, (token_count, token_count), 0)
        column = lax.broadcasted_iota(jnp.int32, (token_count, token_count), 1)
        earlier = (row < column).astype(jnp.bfloat16)
        copies[0].wait()
        first = ids_ref[0:1, :] == expert
        second = ids_ref[1:2, :] == expert
        named = first.astype(jnp.float32) + second.astype(jnp.float32)
        before = jnp.dot(named.astype(jnp.bfloat16), earlier, preferred_element_type=jnp.float32)
        hit_first = jnp.where(first & (before == slot), 1.0, 0.0)
        after_first = before + first.astype(jnp.float32)
        hit_second = jnp.where(second & (after_first == slot), 1.0, 0.0)
        picker = (hit_first + hit_second).astype(jnp.bfloat16)
        copies[1].wait()
        for i in range(steps):
            here = slice(i * tile, (i + 1) * tile)
            copies[2 + i].wait()
            rows = jnp.dot(
                picker, held_ref[:, here], preferred_element_type=jnp.float32
            ).astype(jnp.bfloat16)
            rows_ref[:, here] = rows
            turned_ref[:CAP, here] = rows[CAP:]
            turned_ref[CAP:, here] = rows[:CAP]
        mixer = hit_first * weights_ref[0:1, :] + hit_second * weights_ref[1:2, :]
        high = mixer.astype(jnp.bfloat16).astype(jnp.float32)
        empty = jnp.zeros((LANES - 2 * BLOCK, token_count), jnp.float32)
        stacked = jnp.concatenate([high, mixer - high, empty], axis=0)
        mixer_ref[...] = stacked.T.astype(jnp.bfloat16)

    return call(
        kernel,
        "dispatch",
        [(me, pltpu.SMEM)] + remote(expert_ids.T, route_weights.T, tokens),
        [array(BLOCK, width), array(BLOCK, width), array(token_count, LANES)],
        [
            pltpu.VMEM((2, token_count), expert_ids.dtype),
            pltpu.VMEM((2, token_count), route_weights.dtype),
            pltpu.VMEM((token_count, width), tokens.dtype),
            pltpu.SemaphoreType.DMA((2 + steps,)),
        ],
    )


def call(kernel, name, operands, outs, scratch=(), flops=0, bytes_accessed=0):
    return pl.pallas_call(
        kernel,
        in_specs=[pl.BlockSpec(memory_space=m) for _, m in operands],
        out_specs=[pl.BlockSpec(memory_space=pltpu.VMEM)] * len(outs),
        out_shape=outs,
        scratch_shapes=scratch,
        cost_estimate=pl.CostEstimate(
            flops=flops, bytes_accessed=bytes_accessed, transcendentals=0
        ),
        compiler_params=pltpu.CompilerParams(vmem_limit_bytes=VMEM_LIMIT),
        name=name,
    )(*[v for v, _ in operands])


def local(*values):
    return [(v, pltpu.VMEM) for v in values]


def held(*values):
    return [(pltpu.with_memory_space_constraint(v, pltpu.VMEM), pltpu.VMEM) for v in values]


def remote(*values):
    return [(in_hbm(v), pltpu.HBM) for v in values]


def array(*shape, dtype=jnp.bfloat16):
    return jax.ShapeDtypeStruct(shape, dtype)


def activate(gate, up):
    return (gate / (1.0 + jnp.exp(-gate)) * up).astype(jnp.bfloat16)


def hold_and_multiply(rows, weights, begin, depth, before):
    width = weights.shape[1]
    total = sum(c for _, _, c in rows)
    step = tile_of(depth, 384)
    pieces = depth // step
    before = [] if before is None else [before]

    def kernel(*refs):
        row_refs, (source_ref, *refs) = refs[: len(rows)], refs[len(rows) :]
        held_ref, sum_ref, done = refs[len(before) :]
        copies = [
            pltpu.make_async_copy(
                source_ref.at[pl.ds(begin + i * step, step)],
                held_ref.at[pl.ds(i * step, step)],
                done.at[i],
            )
            for i in range(pieces)
        ]
        for copy in copies:
            copy.start()
        for i, copy in enumerate(copies):
            there = slice(begin + i * step, begin + (i + 1) * step)
            block = jnp.concatenate(
                [r[f : f + c, there] for r, (_, f, c) in zip(row_refs, rows)], axis=0
            )
            copy.wait()
            value = jnp.dot(
                block, held_ref[i * step : (i + 1) * step, :], preferred_element_type=jnp.float32
            )
            if i:
                value += sum_ref[...]
            elif before:
                value += refs[0][...]
            sum_ref[...] = value

    return call(
        kernel,
        "hold_and_multiply",
        local(*[r for r, _, _ in rows]) + remote(weights) + local(*before),
        [pltpu.VMEM((depth, width), weights.dtype), array(total, width, dtype=jnp.float32)],
        [pltpu.SemaphoreType.DMA((pieces,))],
        flops=2 * total * depth * width,
        bytes_accessed=2 * depth * width,
    )


def hidden_of(rows, gates, ups, gate_done=None, up_done=None):
    total = sum(c for _, _, c in rows)
    width = gates[0].shape[1]
    tile = tile_of(width, 1024)
    before = [] if gate_done is None else [gate_done, up_done]

    def kernel(*refs):
        row_refs, refs = refs[: len(rows)], refs[len(rows) :]
        gate_refs, refs = refs[: len(gates)], refs[len(gates) :]
        up_refs, (*before_refs, out_ref) = refs[: len(ups)], refs[len(ups) :]
        block = jnp.concatenate([r[f : f + c, :] for r, (_, f, c) in zip(row_refs, rows)], axis=0)

        @pl.loop(0, width // tile)
        def _(j):
            here = pl.ds(pl.multiple_of(j * tile, tile), tile)
            values = []
            for i, pieces in enumerate((gate_refs, up_refs)):
                known = before_refs[i].shape[0] if before_refs else 0
                value, first = 0.0, 0
                for ref in pieces:
                    last = first + ref.shape[0]
                    value += jnp.dot(
                        block[known:, first:last], ref[:, here], preferred_element_type=jnp.float32
                    )
                    first = last
                if known:
                    value = jnp.concatenate([before_refs[i][:, here], value], axis=0)
                values.append(value)
            out_ref[:, here] = activate(*values)

    depth = sum(g.shape[0] for g in gates)
    return call(
        kernel,
        "hidden",
        local(*[r for r, _, _ in rows]) + held(*gates, *ups) + local(*before),
        [array(total, width)],
        flops=4 * total * depth * width,
        bytes_accessed=4 * depth * width,
    )[0]


def add(value, *others):
    total = value.astype(jnp.float32)
    for other in others:
        total += other.astype(jnp.float32)
    return total.astype(jnp.bfloat16)


def combine(arrived, handed, product, mixer):
    width = arrived.shape[1]
    token_count = mixer.shape[0]
    tile = tile_of(width, 1536)
    steps = width // tile

    def kernel(arrived_ref, handed_ref, product_ref, mixer_ref, out_hbm, mixed_ref, done):
        copies = []
        for i in range(steps):
            here = slice(i * tile, (i + 1) * tile)
            rows = arrived_ref[:, here].astype(jnp.float32) + handed_ref[:, here].astype(
                jnp.float32
            )
            mine = (rows[:CAP] + product_ref[:CAP, here].astype(jnp.float32)).astype(jnp.bfloat16)
            theirs = rows[CAP:].astype(jnp.bfloat16)
            rows = jnp.concatenate([mine, theirs, mine, theirs], axis=0)
            mixed_ref[:, here] = jnp.dot(
                mixer_ref[:, : 2 * BLOCK], rows, preferred_element_type=jnp.float32
            ).astype(jnp.bfloat16)
            copies.append(
                pltpu.make_async_copy(
                    mixed_ref.at[:, pl.ds(i * tile, tile)],
                    out_hbm.at[:, pl.ds(i * tile, tile)],
                    done.at[i],
                )
            )
            copies[i].start()
        for copy in copies:
            copy.wait()

    local_spec = pl.BlockSpec(memory_space=pltpu.VMEM)
    return pl.pallas_call(
        kernel,
        in_specs=[local_spec] * 4,
        out_specs=pl.BlockSpec(memory_space=pltpu.HBM),
        out_shape=array(token_count, width),
        scratch_shapes=[
            pltpu.VMEM((token_count, width), jnp.bfloat16),
            pltpu.SemaphoreType.DMA((steps,)),
        ],
        compiler_params=pltpu.CompilerParams(vmem_limit_bytes=VMEM_LIMIT),
        name="combine",
    )(arrived, handed, product, mixer)


def after(value, other):
    return lax.optimization_barrier((value, other))


def body(tokens, expert_ids, route_weights, w_gate, w_up, w_down):
    ept_count = lax.axis_size("ept")
    hops, across, aside = ring_hops(ept_count, lax.axis_size("exp"))
    reach = ept_count // 2
    w_gate, w_up, w_down = w_gate[0], w_up[0], w_down[0]
    me = lax.axis_index("exp").astype(jnp.int32).reshape(1)

    def hop(value, pairs=hops):
        return lax.ppermute(value, ("ept", "exp"), pairs)

    own, turned, mixer = dispatch(me, expert_ids, route_weights, tokens)
    units = [own, swap(turned)]
    arriving = [hop(units[0]), hop(units[1])]
    plan = [(0, 0, 3, 2, 3, 3), (0, 3, 6, 3, 3, 4), (0, 6, 8, 4, 3, 5), (1, 0, 3, 5, 6, 6), (1, 3, 8, 6, 6, 8)] if ept_count == 8 else []
    weights, held_weights, sums, todo = [w_up, w_gate], [[], []], [None, None], []
    given = [None]
    while len(units) < 2 * reach + 1:
        unit = arriving[len(units) - 2]
        for i, before in list(todo):
            if before == len(units):
                unit, sums[i] = after(unit, sums[i])
                todo.remove((i, before))
        units.append(unit)
        if len(arriving) < 2 * reach - 1:
            arriving.append(hop(unit))
        for i, first, last, newest, count, before in plan:
            if newest == len(units) - 1:
                units[-1], source = after(units[-1], weights[i])
                eighth = source.shape[0] // 8
                rows = [(u, 0, CAP) for u in units[:count]]
                if given[-1] is not None and i == 1:
                    source, given[-1] = after(source, given[-1])
                piece, sums[i] = hold_and_multiply(
                    rows, source, first * eighth, (last - first) * eighth, sums[i]
                )
                held_weights[i].append(piece)
                todo.append((i, before))
        if len(units) == 2 * reach - 2:
            given = [swap(jnp.concatenate([u[CAP:] for u in units[2:]], axis=0))]
    given.append(swap(jnp.concatenate([u[CAP:] for u in units[-3:-1]], axis=0)))
    far = swap(units[-1][CAP:])
    ups, gates = (h if h else [w] for h, w in zip(held_weights, weights))
    up_done, gate_done = sums

    rows = [(u, 0, CAP) for u in units[:-1]]
    rows += [(given[0], BLOCK * k, BLOCK) for k in range(reach - 2)] + [(given[1], 0, BLOCK)]
    rows += [(units[-1], 0, CAP), (far, 0, CAP)]
    groups = [[]]
    for row in rows:
        if sum(c for _, _, c in groups[-1]) + row[2] > ROWS:
            groups.append([])
        groups[-1].append(row)
    hidden = [hidden_of(groups[0], gates, ups, gate_done, up_done)]
    hidden += [hidden_of(group, gates, ups) for group in groups[1:]]
    hidden = jnp.concatenate(hidden, axis=0) if len(hidden) > 1 else hidden[0]
    mine = [hidden[BLOCK * k : BLOCK * (k + 1)] for k in range(reach)]
    others = [hidden[BLOCK * k : BLOCK * (k + 1)] for k in range(reach, 2 * reach)]

    def product_of(*parts):
        product = jnp.dot(
            jnp.concatenate(parts, axis=0), w_down, preferred_element_type=jnp.float32
        )
        return lax.optimization_barrier(product.astype(jnp.bfloat16))

    product = product_of(mine[reach - 1], *others[-2:])
    handed, kept = [swap(product[:BLOCK])], [product[BLOCK : 2 * BLOCK]]
    a = [hop(product[2 * BLOCK : 2 * BLOCK + CAP]), hop(product[2 * BLOCK + CAP :], aside)]
    first = jnp.concatenate([kept[0][:CAP], handed[0][:CAP]], axis=0)
    first, parts = after(first, (*mine[:-1], *others[:-2]))
    product = product_of(*parts)
    a, product = after(a, product)
    own = product[:BLOCK]
    if reach > 2:
        more = swap(product[BLOCK : BLOCK * (reach - 1)])
        handed += [more[BLOCK * k : BLOCK * (k + 1)] for k in reversed(range(reach - 2))]
        more = product[BLOCK * (reach - 1) :]
        kept += [more[BLOCK * k : BLOCK * (k + 1)] for k in reversed(range(reach - 2))]
    b = None
    for mine, theirs in zip(kept, handed):
        unit = jnp.concatenate([mine[:CAP], theirs[:CAP]], axis=0)
        b = hop(first if b is None else add(unit, b))
        if isinstance(a, list):
            a = jnp.concatenate(a, axis=0)
        a = hop(add(jnp.concatenate([mine[CAP:], theirs[CAP:]], axis=0), a))
    handover = swap(jnp.concatenate([b[CAP:], add(b[:CAP], own[CAP:])], axis=0))
    return combine(a, handover, own[:CAP], mixer)


def solution(mesh):
    placed = (
        P(("groups", "ept", "exp"), None),
        P(("groups", "ept", "exp"), None),
        P(("groups", "ept", "exp"), None),
        P("exp", None, "ept"),
        P("exp", None, "ept"),
        P("exp", "ept", None),
    )
    return jax.shard_map(
        body,
        mesh=mesh,
        in_specs=placed,
        out_specs=P(("groups", "ept", "exp"), None),
        check_vma=False,
    )
```

```python
import jax
import jax.numpy as jnp
from jax import lax
from jax.experimental import pallas as pl
from jax.experimental.pallas import tpu as pltpu
from jax.sharding import PartitionSpec as P

CAP = 16
BLOCK = 2 * CAP
LANES = 128
ROWS = 256
VMEM_LIMIT = 8 * 1024 * 1024


def ring_hops(count, cores):
    cycle = [0, 2, 4, 6, 7, 5, 3, 1] if count == 8 else list(range(count))
    hops, across, aside = [], [], []
    for here, there in zip(cycle, cycle[1:] + cycle[:1]):
        for core, (begin, end) in enumerate(((here, there), (there, here))):
            hops.append((begin * cores + core, end * cores + core))
            across.append((begin * cores + core, end * cores + 1 - core))
            aside.append((begin * cores + 1 - core, end * cores + core))
    return hops, across, aside


def swap(value):
    return lax.ppermute(value, "exp", [(0, 1), (1, 0)])


def tile_of(size, most):
    return max(t for t in range(LANES, most + 1, LANES) if size % t == 0)


def in_hbm(value):
    return pltpu.with_memory_space_constraint(value, pltpu.HBM)


def dispatch(me, expert_ids, route_weights, tokens):
    token_count, width = tokens.shape
    tile = tile_of(width, 3072)
    steps = width // tile

    def kernel(me_ref, ids_hbm, weights_hbm, tokens_hbm, rows_ref, turned_ref, mixer_ref, *scratch):
        ids_ref, weights_ref, held_ref, done = scratch
        copies = [
            pltpu.make_async_copy(ids_hbm, ids_ref, done.at[0]),
            pltpu.make_async_copy(weights_hbm, weights_ref, done.at[1]),
        ]
        for i in range(steps):
            here = pl.ds(i * tile, tile)
            copies.append(
                pltpu.make_async_copy(
                    tokens_hbm.at[:, here], held_ref.at[:, here], done.at[2 + i]
                )
            )
        for copy in copies:
            copy.start()
        line = lax.broadcasted_iota(jnp.int32, (BLOCK, token_count), 0)
        expert = (line // CAP + me_ref[0]) % 2
        slot = (line % CAP).astype(jnp.float32)
        row = lax.broadcasted_iota(jnp.int32, (token_count, token_count), 0)
        column = lax.broadcasted_iota(jnp.int32, (token_count, token_count), 1)
        earlier = (row < column).astype(jnp.bfloat16)
        copies[0].wait()
        first = ids_ref[0:1, :] == expert
        second = ids_ref[1:2, :] == expert
        named = first.astype(jnp.float32) + second.astype(jnp.float32)
        before = jnp.dot(named.astype(jnp.bfloat16), earlier, preferred_element_type=jnp.float32)
        hit_first = jnp.where(first & (before == slot), 1.0, 0.0)
        after_first = before + first.astype(jnp.float32)
        hit_second = jnp.where(second & (after_first == slot), 1.0, 0.0)
        picker = (hit_first + hit_second).astype(jnp.bfloat16)
        copies[1].wait()
        for i in range(steps):
            here = slice(i * tile, (i + 1) * tile)
            copies[2 + i].wait()
            rows = jnp.dot(
                picker, held_ref[:, here], preferred_element_type=jnp.float32
            ).astype(jnp.bfloat16)
            rows_ref[:, here] = rows
            turned_ref[:CAP, here] = rows[CAP:]
            turned_ref[CAP:, here] = rows[:CAP]
        mixer = hit_first * weights_ref[0:1, :] + hit_second * weights_ref[1:2, :]
        high = mixer.astype(jnp.bfloat16).astype(jnp.float32)
        empty = jnp.zeros((LANES - 2 * BLOCK, token_count), jnp.float32)
        stacked = jnp.concatenate([high, mixer - high, empty], axis=0)
        mixer_ref[...] = stacked.T.astype(jnp.bfloat16)

    return call(
        kernel,
        "dispatch",
        [(me, pltpu.SMEM)] + remote(expert_ids.T, route_weights.T, tokens),
        [array(BLOCK, width), array(BLOCK, width), array(token_count, LANES)],
        [
            pltpu.VMEM((2, token_count), expert_ids.dtype),
            pltpu.VMEM((2, token_count), route_weights.dtype),
            pltpu.VMEM((token_count, width), tokens.dtype),
            pltpu.SemaphoreType.DMA((2 + steps,)),
        ],
    )


def call(kernel, name, operands, outs, scratch=(), flops=0, bytes_accessed=0):
    return pl.pallas_call(
        kernel,
        in_specs=[pl.BlockSpec(memory_space=m) for _, m in operands],
        out_specs=[pl.BlockSpec(memory_space=pltpu.VMEM)] * len(outs),
        out_shape=outs,
        scratch_shapes=scratch,
        cost_estimate=pl.CostEstimate(
            flops=flops, bytes_accessed=bytes_accessed, transcendentals=0
        ),
        compiler_params=pltpu.CompilerParams(vmem_limit_bytes=VMEM_LIMIT),
        name=name,
    )(*[v for v, _ in operands])


def local(*values):
    return [(v, pltpu.VMEM) for v in values]


def held(*values):
    return [(pltpu.with_memory_space_constraint(v, pltpu.VMEM), pltpu.VMEM) for v in values]


def remote(*values):
    return [(in_hbm(v), pltpu.HBM) for v in values]


def array(*shape, dtype=jnp.bfloat16):
    return jax.ShapeDtypeStruct(shape, dtype)


def activate(gate, up):
    return (gate / (1.0 + jnp.exp(-gate)) * up).astype(jnp.bfloat16)


def hold_and_multiply(rows, weights, begin, depth, before):
    width = weights.shape[1]
    total = sum(c for _, _, c in rows)
    step = tile_of(depth, 384)
    pieces = depth // step
    before = [] if before is None else [before]

    def kernel(*refs):
        row_refs, (source_ref, *refs) = refs[: len(rows)], refs[len(rows) :]
        held_ref, sum_ref, done = refs[len(before) :]
        copies = [
            pltpu.make_async_copy(
                source_ref.at[pl.ds(begin + i * step, step)],
                held_ref.at[pl.ds(i * step, step)],
                done.at[i],
            )
            for i in range(pieces)
        ]
        for copy in copies:
            copy.start()
        for i, copy in enumerate(copies):
            there = slice(begin + i * step, begin + (i + 1) * step)
            block = jnp.concatenate(
                [r[f : f + c, there] for r, (_, f, c) in zip(row_refs, rows)], axis=0
            )
            copy.wait()
            value = jnp.dot(
                block, held_ref[i * step : (i + 1) * step, :], preferred_element_type=jnp.float32
            )
            if i:
                value += sum_ref[...]
            elif before:
                value += refs[0][...]
            sum_ref[...] = value

    return call(
        kernel,
        "hold_and_multiply",
        local(*[r for r, _, _ in rows]) + remote(weights) + local(*before),
        [pltpu.VMEM((depth, width), weights.dtype), array(total, width, dtype=jnp.float32)],
        [pltpu.SemaphoreType.DMA((pieces,))],
        flops=2 * total * depth * width,
        bytes_accessed=2 * depth * width,
    )


def hidden_of(rows, gates, ups, gate_done=None, up_done=None):
    total = sum(c for _, _, c in rows)
    width = gates[0].shape[1]
    tile = tile_of(width, 1024)
    before = [] if gate_done is None else [gate_done, up_done]

    def kernel(*refs):
        row_refs, refs = refs[: len(rows)], refs[len(rows) :]
        gate_refs, refs = refs[: len(gates)], refs[len(gates) :]
        up_refs, (*before_refs, out_ref) = refs[: len(ups)], refs[len(ups) :]
        block = jnp.concatenate([r[f : f + c, :] for r, (_, f, c) in zip(row_refs, rows)], axis=0)

        @pl.loop(0, width // tile)
        def _(j):
            here = pl.ds(pl.multiple_of(j * tile, tile), tile)
            values = []
            for i, pieces in enumerate((gate_refs, up_refs)):
                known = before_refs[i].shape[0] if before_refs else 0
                value, first = 0.0, 0
                for ref in pieces:
                    last = first + ref.shape[0]
                    value += jnp.dot(
                        block[known:, first:last], ref[:, here], preferred_element_type=jnp.float32
                    )
                    first = last
                if known:
                    value = jnp.concatenate([before_refs[i][:, here], value], axis=0)
                values.append(value)
            out_ref[:, here] = activate(*values)

    depth = sum(g.shape[0] for g in gates)
    return call(
        kernel,
        "hidden",
        local(*[r for r, _, _ in rows]) + held(*gates, *ups) + local(*before),
        [array(total, width)],
        flops=4 * total * depth * width,
        bytes_accessed=4 * depth * width,
    )[0]


def add(value, *others):
    total = value.astype(jnp.float32)
    for other in others:
        total += other.astype(jnp.float32)
    return total.astype(jnp.bfloat16)


def combine(arrived, handed, product, mixer):
    width = arrived.shape[1]
    token_count = mixer.shape[0]
    tile = tile_of(width, 1536)
    steps = width // tile

    def kernel(arrived_ref, handed_ref, product_ref, mixer_ref, out_hbm, mixed_ref, done):
        copies = []
        for i in range(steps):
            here = slice(i * tile, (i + 1) * tile)
            rows = arrived_ref[:, here].astype(jnp.float32) + handed_ref[:, here].astype(
                jnp.float32
            )
            mine = (rows[:CAP] + product_ref[:CAP, here].astype(jnp.float32)).astype(jnp.bfloat16)
            theirs = rows[CAP:].astype(jnp.bfloat16)
            rows = jnp.concatenate([mine, theirs, mine, theirs], axis=0)
            mixed_ref[:, here] = jnp.dot(
                mixer_ref[:, : 2 * BLOCK], rows, preferred_element_type=jnp.float32
            ).astype(jnp.bfloat16)
            copies.append(
                pltpu.make_async_copy(
                    mixed_ref.at[:, pl.ds(i * tile, tile)],
                    out_hbm.at[:, pl.ds(i * tile, tile)],
                    done.at[i],
                )
            )
            copies[i].start()
        for copy in copies:
            copy.wait()

    local_spec = pl.BlockSpec(memory_space=pltpu.VMEM)
    return pl.pallas_call(
        kernel,
        in_specs=[local_spec] * 4,
        out_specs=pl.BlockSpec(memory_space=pltpu.HBM),
        out_shape=array(token_count, width),
        scratch_shapes=[
            pltpu.VMEM((token_count, width), jnp.bfloat16),
            pltpu.SemaphoreType.DMA((steps,)),
        ],
        compiler_params=pltpu.CompilerParams(vmem_limit_bytes=VMEM_LIMIT),
        name="combine",
    )(arrived, handed, product, mixer)


def after(value, other):
    return lax.optimization_barrier((value, other))


def body(tokens, expert_ids, route_weights, w_gate, w_up, w_down):
    ept_count = lax.axis_size("ept")
    hops, across, aside = ring_hops(ept_count, lax.axis_size("exp"))
    reach = ept_count // 2
    w_gate, w_up, w_down = w_gate[0], w_up[0], w_down[0]
    me = lax.axis_index("exp").astype(jnp.int32).reshape(1)

    def hop(value, pairs=hops):
        return lax.ppermute(value, ("ept", "exp"), pairs)

    own, turned, mixer = dispatch(me, expert_ids, route_weights, tokens)
    units = [own, swap(turned)]
    arriving = [hop(units[0]), hop(units[1])]
    plan = [(0, 0, 3, 2, 3, 3), (0, 3, 6, 3, 3, 4), (0, 6, 8, 4, 3, 5), (1, 0, 3, 5, 6, 6), (1, 3, 8, 6, 6, 8)] if ept_count == 8 else []
    weights, held_weights, sums, todo = [w_up, w_gate], [[], []], [None, None], []
    given = [None]
    while len(units) < 2 * reach + 1:
        unit = arriving[len(units) - 2]
        for i, before in list(todo):
            if before == len(units):
                unit, sums[i] = after(unit, sums[i])
                todo.remove((i, before))
        units.append(unit)
        if len(arriving) < 2 * reach - 1:
            arriving.append(hop(unit))
        for i, first, last, newest, count, before in plan:
            if newest == len(units) - 1:
                units[-1], source = after(units[-1], weights[i])
                eighth = source.shape[0] // 8
                rows = [(u, 0, CAP) for u in units[:count]]
                if given[-1] is not None and i == 1:
                    source, given[-1] = after(source, given[-1])
                piece, sums[i] = hold_and_multiply(
                    rows, source, first * eighth, (last - first) * eighth, sums[i]
                )
                held_weights[i].append(piece)
                todo.append((i, before))
        if len(units) == 2 * reach - 2:
            given = [swap(jnp.concatenate([u[CAP:] for u in units[2:]], axis=0))]
    given.append(swap(jnp.concatenate([u[CAP:] for u in units[-3:-1]], axis=0)))
    far = swap(units[-1][CAP:])
    ups, gates = (h if h else [w] for h, w in zip(held_weights, weights))
    up_done, gate_done = sums

    rows = [(u, 0, CAP) for u in units[:-3]]
    rows += [(given[0], BLOCK * k, BLOCK) for k in range(reach - 2)]
    rows += [(u, 0, CAP) for u in units[-3:-1]] + [(given[1], 0, BLOCK)]
    rows += [(units[-1], 0, CAP), (far, 0, CAP)]
    groups = [[]]
    for row in rows:
        if sum(c for _, _, c in groups[-1]) + row[2] > ROWS:
            groups.append([])
        groups[-1].append(row)
    hidden = [hidden_of(groups[0], gates, ups, gate_done, up_done)]
    hidden += [hidden_of(group, gates, ups) for group in groups[1:]]
    hidden = jnp.concatenate(hidden, axis=0) if len(hidden) > 1 else hidden[0]
    def product_of(part):
        product = jnp.dot(part, w_down, preferred_element_type=jnp.float32)
        return lax.optimization_barrier(product.astype(jnp.bfloat16))

    product = product_of(hidden[-3 * BLOCK :])
    handed, kept = [swap(product[:BLOCK])], [product[BLOCK : 2 * BLOCK]]
    a = [hop(product[2 * BLOCK : 2 * BLOCK + CAP]), hop(product[2 * BLOCK + CAP :], aside)]
    first = jnp.concatenate([kept[0][:CAP], handed[0][:CAP]], axis=0)
    first, part = after(first, hidden[: -3 * BLOCK])
    product = product_of(part)
    a, product = after(a, product)
    own = product[:BLOCK]
    if reach > 2:
        more = swap(product[BLOCK : BLOCK * (reach - 1)])
        handed += [more[BLOCK * k : BLOCK * (k + 1)] for k in reversed(range(reach - 2))]
        more = product[BLOCK * (reach - 1) :]
        kept += [more[BLOCK * k : BLOCK * (k + 1)] for k in reversed(range(reach - 2))]
    b = None
    for mine, theirs in zip(kept, handed):
        unit = jnp.concatenate([mine[:CAP], theirs[:CAP]], axis=0)
        b = hop(first if b is None else add(unit, b))
        if isinstance(a, list):
            a = jnp.concatenate(a, axis=0)
        a = hop(add(jnp.concatenate([mine[CAP:], theirs[CAP:]], axis=0), a))
    handover = swap(jnp.concatenate([b[CAP:], add(b[:CAP], own[CAP:])], axis=0))
    return combine(a, handover, own[:CAP], mixer)


def solution(mesh):
    placed = (
        P(("groups", "ept", "exp"), None),
        P(("groups", "ept", "exp"), None),
        P(("groups", "ept", "exp"), None),
        P("exp", None, "ept"),
        P("exp", None, "ept"),
        P("exp", "ept", None),
    )
    return jax.shard_map(
        body,
        mesh=mesh,
        in_specs=placed,
        out_specs=P(("groups", "ept", "exp"), None),
        check_vma=False,
    )
```

```python
import jax
import jax.numpy as jnp
from jax import lax
from jax.experimental import pallas as pl
from jax.experimental.pallas import tpu as pltpu
from jax.sharding import PartitionSpec as P

CAP = 16
BLOCK = 2 * CAP
LANES = 128
ROWS = 256
VMEM_LIMIT = 8 * 1024 * 1024


def ring_hops(count, cores):
    cycle = [0, 2, 4, 6, 7, 5, 3, 1] if count == 8 else list(range(count))
    hops, across, aside = [], [], []
    for here, there in zip(cycle, cycle[1:] + cycle[:1]):
        for core, (begin, end) in enumerate(((here, there), (there, here))):
            hops.append((begin * cores + core, end * cores + core))
            across.append((begin * cores + core, end * cores + 1 - core))
            aside.append((begin * cores + 1 - core, end * cores + core))
    return hops, across, aside


def swap(value):
    return lax.ppermute(value, "exp", [(0, 1), (1, 0)])


def tile_of(size, most):
    return max(t for t in range(LANES, most + 1, LANES) if size % t == 0)


def in_hbm(value):
    return pltpu.with_memory_space_constraint(value, pltpu.HBM)


def dispatch(me, expert_ids, route_weights, tokens):
    token_count, width = tokens.shape
    tile = tile_of(width, 3072)
    steps = width // tile

    def kernel(me_ref, ids_hbm, weights_hbm, tokens_hbm, rows_ref, turned_ref, mixer_ref, *scratch):
        ids_ref, weights_ref, held_ref, done = scratch
        copies = [
            pltpu.make_async_copy(ids_hbm, ids_ref, done.at[0]),
            pltpu.make_async_copy(weights_hbm, weights_ref, done.at[1]),
        ]
        for i in range(steps):
            here = pl.ds(i * tile, tile)
            copies.append(
                pltpu.make_async_copy(
                    tokens_hbm.at[:, here], held_ref.at[:, here], done.at[2 + i]
                )
            )
        for copy in copies:
            copy.start()
        line = lax.broadcasted_iota(jnp.int32, (BLOCK, token_count), 0)
        expert = (line // CAP + me_ref[0]) % 2
        slot = (line % CAP).astype(jnp.float32)
        row = lax.broadcasted_iota(jnp.int32, (token_count, token_count), 0)
        column = lax.broadcasted_iota(jnp.int32, (token_count, token_count), 1)
        earlier = (row < column).astype(jnp.bfloat16)
        copies[0].wait()
        first = ids_ref[0:1, :] == expert
        second = ids_ref[1:2, :] == expert
        named = first.astype(jnp.float32) + second.astype(jnp.float32)
        before = jnp.dot(named.astype(jnp.bfloat16), earlier, preferred_element_type=jnp.float32)
        hit_first = jnp.where(first & (before == slot), 1.0, 0.0)
        after_first = before + first.astype(jnp.float32)
        hit_second = jnp.where(second & (after_first == slot), 1.0, 0.0)
        picker = (hit_first + hit_second).astype(jnp.bfloat16)
        copies[1].wait()
        for i in range(steps):
            here = slice(i * tile, (i + 1) * tile)
            copies[2 + i].wait()
            rows = jnp.dot(
                picker, held_ref[:, here], preferred_element_type=jnp.float32
            ).astype(jnp.bfloat16)
            rows_ref[:, here] = rows
            turned_ref[:CAP, here] = rows[CAP:]
            turned_ref[CAP:, here] = rows[:CAP]
        mixer = hit_first * weights_ref[0:1, :] + hit_second * weights_ref[1:2, :]
        high = mixer.astype(jnp.bfloat16).astype(jnp.float32)
        empty = jnp.zeros((LANES - 2 * BLOCK, token_count), jnp.float32)
        stacked = jnp.concatenate([high, mixer - high, empty], axis=0)
        mixer_ref[...] = stacked.T.astype(jnp.bfloat16)

    return call(
        kernel,
        "dispatch",
        [(me, pltpu.SMEM)] + remote(expert_ids.T, route_weights.T, tokens),
        [array(BLOCK, width), array(BLOCK, width), array(token_count, LANES)],
        [
            pltpu.VMEM((2, token_count), expert_ids.dtype),
            pltpu.VMEM((2, token_count), route_weights.dtype),
            pltpu.VMEM((token_count, width), tokens.dtype),
            pltpu.SemaphoreType.DMA((2 + steps,)),
        ],
    )


def call(kernel, name, operands, outs, scratch=(), flops=0, bytes_accessed=0):
    return pl.pallas_call(
        kernel,
        in_specs=[pl.BlockSpec(memory_space=m) for _, m in operands],
        out_specs=[pl.BlockSpec(memory_space=pltpu.VMEM)] * len(outs),
        out_shape=outs,
        scratch_shapes=scratch,
        cost_estimate=pl.CostEstimate(
            flops=flops, bytes_accessed=bytes_accessed, transcendentals=0
        ),
        compiler_params=pltpu.CompilerParams(vmem_limit_bytes=VMEM_LIMIT),
        name=name,
    )(*[v for v, _ in operands])


def local(*values):
    return [(v, pltpu.VMEM) for v in values]


def held(*values):
    return [(pltpu.with_memory_space_constraint(v, pltpu.VMEM), pltpu.VMEM) for v in values]


def remote(*values):
    return [(in_hbm(v), pltpu.HBM) for v in values]


def array(*shape, dtype=jnp.bfloat16):
    return jax.ShapeDtypeStruct(shape, dtype)


def activate(gate, up):
    return (gate / (1.0 + jnp.exp(-gate)) * up).astype(jnp.bfloat16)


def hold_and_multiply(rows, weights, begin, depth, before):
    width = weights.shape[1]
    total = sum(c for _, _, c in rows)
    step = tile_of(depth, 384)
    pieces = depth // step
    before = [] if before is None else [before]

    def kernel(*refs):
        row_refs, (source_ref, *refs) = refs[: len(rows)], refs[len(rows) :]
        held_ref, sum_ref, done = refs[len(before) :]
        copies = [
            pltpu.make_async_copy(
                source_ref.at[pl.ds(begin + i * step, step)],
                held_ref.at[pl.ds(i * step, step)],
                done.at[i],
            )
            for i in range(pieces)
        ]
        for copy in copies:
            copy.start()
        for i, copy in enumerate(copies):
            there = slice(begin + i * step, begin + (i + 1) * step)
            block = jnp.concatenate(
                [r[f : f + c, there] for r, (_, f, c) in zip(row_refs, rows)], axis=0
            )
            copy.wait()
            value = jnp.dot(
                block, held_ref[i * step : (i + 1) * step, :], preferred_element_type=jnp.float32
            )
            if i:
                value += sum_ref[...]
            elif before:
                value += refs[0][...]
            sum_ref[...] = value

    return call(
        kernel,
        "hold_and_multiply",
        local(*[r for r, _, _ in rows]) + remote(weights) + local(*before),
        [pltpu.VMEM((depth, width), weights.dtype), array(total, width, dtype=jnp.float32)],
        [pltpu.SemaphoreType.DMA((pieces,))],
        flops=2 * total * depth * width,
        bytes_accessed=2 * depth * width,
    )


def hidden_of(rows, gates, ups, gate_done=None, up_done=None):
    total = sum(c for _, _, c in rows)
    width = gates[0].shape[1]
    tile = tile_of(width, 1024)
    before = [] if gate_done is None else [gate_done, up_done]

    def kernel(*refs):
        row_refs, refs = refs[: len(rows)], refs[len(rows) :]
        gate_refs, refs = refs[: len(gates)], refs[len(gates) :]
        up_refs, (*before_refs, out_ref) = refs[: len(ups)], refs[len(ups) :]
        block = jnp.concatenate([r[f : f + c, :] for r, (_, f, c) in zip(row_refs, rows)], axis=0)

        @pl.loop(0, width // tile)
        def _(j):
            here = pl.ds(pl.multiple_of(j * tile, tile), tile)
            values = []
            for i, pieces in enumerate((gate_refs, up_refs)):
                known = before_refs[i].shape[0] if before_refs else 0
                value, first = 0.0, 0
                for ref in pieces:
                    last = first + ref.shape[0]
                    value += jnp.dot(
                        block[known:, first:last], ref[:, here], preferred_element_type=jnp.float32
                    )
                    first = last
                if known:
                    value = jnp.concatenate([before_refs[i][:, here], value], axis=0)
                values.append(value)
            out_ref[:, here] = activate(*values)

    depth = sum(g.shape[0] for g in gates)
    return call(
        kernel,
        "hidden",
        local(*[r for r, _, _ in rows]) + held(*gates, *ups) + local(*before),
        [array(total, width)],
        flops=4 * total * depth * width,
        bytes_accessed=4 * depth * width,
    )[0]


def add(value, *others):
    total = value.astype(jnp.float32)
    for other in others:
        total += other.astype(jnp.float32)
    return total.astype(jnp.bfloat16)


def combine(arrived, handed, product, mixer):
    width = arrived.shape[1]
    token_count = mixer.shape[0]
    tile = tile_of(width, 3072)
    steps = width // tile

    def kernel(arrived_ref, handed_ref, product_ref, mixer_ref, out_hbm, mixed_ref, done):
        copies = []
        for i in range(steps):
            here = slice(i * tile, (i + 1) * tile)
            rows = arrived_ref[:, here].astype(jnp.float32) + handed_ref[:, here].astype(
                jnp.float32
            )
            mine = (rows[:CAP] + product_ref[:CAP, here].astype(jnp.float32)).astype(jnp.bfloat16)
            theirs = rows[CAP:].astype(jnp.bfloat16)
            rows = jnp.concatenate([mine, theirs, mine, theirs], axis=0)
            mixed_ref[:, here] = jnp.dot(
                mixer_ref[:, : 2 * BLOCK], rows, preferred_element_type=jnp.float32
            ).astype(jnp.bfloat16)
            copies.append(
                pltpu.make_async_copy(
                    mixed_ref.at[:, pl.ds(i * tile, tile)],
                    out_hbm.at[:, pl.ds(i * tile, tile)],
                    done.at[i],
                )
            )
            copies[i].start()
        for copy in copies:
            copy.wait()

    local_spec = pl.BlockSpec(memory_space=pltpu.VMEM)
    return pl.pallas_call(
        kernel,
        in_specs=[local_spec] * 4,
        out_specs=pl.BlockSpec(memory_space=pltpu.HBM),
        out_shape=array(token_count, width),
        scratch_shapes=[
            pltpu.VMEM((token_count, width), jnp.bfloat16),
            pltpu.SemaphoreType.DMA((steps,)),
        ],
        compiler_params=pltpu.CompilerParams(vmem_limit_bytes=VMEM_LIMIT),
        name="combine",
    )(arrived, handed, product, mixer)


def after(value, other):
    return lax.optimization_barrier((value, other))


def body(tokens, expert_ids, route_weights, w_gate, w_up, w_down):
    ept_count = lax.axis_size("ept")
    hops, across, aside = ring_hops(ept_count, lax.axis_size("exp"))
    reach = ept_count // 2
    w_gate, w_up, w_down = w_gate[0], w_up[0], w_down[0]
    me = lax.axis_index("exp").astype(jnp.int32).reshape(1)

    def hop(value, pairs=hops):
        return lax.ppermute(value, ("ept", "exp"), pairs)

    own, turned, mixer = dispatch(me, expert_ids, route_weights, tokens)
    units = [own, swap(turned)]
    arriving = [hop(units[0]), hop(units[1])]
    plan = [(0, 0, 3, 2, 3, 3), (0, 3, 6, 3, 3, 4), (0, 6, 8, 4, 3, 5), (1, 0, 3, 5, 6, 6), (1, 3, 8, 6, 6, 8)] if ept_count == 8 else []
    weights, held_weights, sums, todo = [w_up, w_gate], [[], []], [None, None], []
    given = [None]
    while len(units) < 2 * reach + 1:
        unit = arriving[len(units) - 2]
        for i, before in list(todo):
            if before == len(units):
                unit, sums[i] = after(unit, sums[i])
                todo.remove((i, before))
        units.append(unit)
        if len(arriving) < 2 * reach - 1:
            arriving.append(hop(unit))
        for i, first, last, newest, count, before in plan:
            if newest == len(units) - 1:
                units[-1], source = after(units[-1], weights[i])
                eighth = source.shape[0] // 8
                rows = [(u, 0, CAP) for u in units[:count]]
                if given[-1] is not None and i == 1:
                    source, given[-1] = after(source, given[-1])
                piece, sums[i] = hold_and_multiply(
                    rows, source, first * eighth, (last - first) * eighth, sums[i]
                )
                held_weights[i].append(piece)
                todo.append((i, before))
        if len(units) == 2 * reach - 2:
            given = [swap(jnp.concatenate([u[CAP:] for u in units[2:]], axis=0))]
    given.append(swap(jnp.concatenate([u[CAP:] for u in units[-3:-1]], axis=0)))
    far = swap(units[-1][CAP:])
    ups, gates = (h if h else [w] for h, w in zip(held_weights, weights))
    up_done, gate_done = sums

    rows = [(u, 0, CAP) for u in units[:-3]]
    rows += [(given[0], BLOCK * k, BLOCK) for k in range(reach - 2)]
    rows += [(u, 0, CAP) for u in units[-3:-1]] + [(given[1], 0, BLOCK)]
    rows += [(units[-1], 0, CAP), (far, 0, CAP)]
    groups = [[]]
    for row in rows:
        if sum(c for _, _, c in groups[-1]) + row[2] > ROWS:
            groups.append([])
        groups[-1].append(row)
    hidden = [hidden_of(groups[0], gates, ups, gate_done, up_done)]
    hidden += [hidden_of(group, gates, ups) for group in groups[1:]]
    hidden = jnp.concatenate(hidden, axis=0) if len(hidden) > 1 else hidden[0]
    def product_of(part):
        product = jnp.dot(part, w_down, preferred_element_type=jnp.float32)
        return lax.optimization_barrier(product.astype(jnp.bfloat16))

    product = product_of(hidden[-3 * BLOCK :])
    handed, kept = [swap(product[:BLOCK])], [product[BLOCK : 2 * BLOCK]]
    a = [hop(product[2 * BLOCK : 2 * BLOCK + CAP]), hop(product[2 * BLOCK + CAP :], aside)]
    first = jnp.concatenate([kept[0][:CAP], handed[0][:CAP]], axis=0)
    first, part = after(first, hidden[: -3 * BLOCK])
    product = product_of(part)
    a, product = after(a, product)
    own = product[:BLOCK]
    if reach > 2:
        more = swap(product[BLOCK : BLOCK * (reach - 1)])
        handed += [more[BLOCK * k : BLOCK * (k + 1)] for k in reversed(range(reach - 2))]
        more = product[BLOCK * (reach - 1) :]
        kept += [more[BLOCK * k : BLOCK * (k + 1)] for k in reversed(range(reach - 2))]
    b = None
    for mine, theirs in zip(kept, handed):
        unit = jnp.concatenate([mine[:CAP], theirs[:CAP]], axis=0)
        b = hop(first if b is None else add(unit, b))
        if isinstance(a, list):
            a = jnp.concatenate(a, axis=0)
        a = hop(add(jnp.concatenate([mine[CAP:], theirs[CAP:]], axis=0), a))
    handover = swap(jnp.concatenate([b[CAP:], add(b[:CAP], own[CAP:])], axis=0))
    return combine(a, handover, own[:CAP], mixer)


def solution(mesh):
    placed = (
        P(("groups", "ept", "exp"), None),
        P(("groups", "ept", "exp"), None),
        P(("groups", "ept", "exp"), None),
        P("exp", None, "ept"),
        P("exp", None, "ept"),
        P("exp", "ept", None),
    )
    return jax.shard_map(
        body,
        mesh=mesh,
        in_specs=placed,
        out_specs=P(("groups", "ept", "exp"), None),
        check_vma=False,
    )
```
